256 devices in a mesh: group: 8 (over x_lo, y), shard: 32 (over z, x_hi, core).
Axes of the slice: x: 4 (x_hi: 2, x_lo: 2; x = x_hi * 2 + x_lo), y: 4, z: 8, core: 2. Of those that a mesh axis runs over, the one named last changes fastest.
Arguments:
- weights: bfloat16 [8, 10240, 7168], P('group', 'shard'), may hold values from -64 to 64
- factor_init: float32 [8, 16, 7168], P('group'), may hold values from -6 to 6
Outputs:
- new_weights: bfloat16 [8, 10240, 7168], P('group', 'shard')
- next_factor: float32 [8, 16, 7168], P('group')
The draws below stay inside these ranges and needn't reach their ends.
All inputs are finite; a program needn't handle non-finite values.
Results may differ from the reference program's by a relative error of at most 0.0051.
Values may be sent and summed in bfloat16 or wider, within the bound.
A program may use at most 64 MiB of HBM per device.

```python
import jax
import jax.numpy as jnp
from jax import lax

D = 7168
FF = 10240
R = 16
STEPS = 2
GROUPS = 8


def draw_weights(key, part):
    key = jax.random.fold_in(key, 11)
    noise_key, row_key, col_key = jax.random.split(key, 3)
    shape = (GROUPS, FF, D)
    position = jnp.arange(FF, dtype=jnp.float32) / FF
    row_spread = jax.random.uniform(row_key, (GROUPS, FF, 1), jnp.float32)
    col_spread = jax.random.uniform(col_key, (GROUPS, 1, D), jnp.float32)
    scale = 0.2 * jnp.power(3.0, position)[None, :, None] * jnp.power(10.0, 0.5 * (row_spread - 0.5)) * jnp.power(2.0, col_spread - 0.5)
    noise = jnp.clip(jax.random.normal(noise_key, shape, jnp.float32), -5.0, 5.0)
    values = noise * scale
    return values.astype(jnp.bfloat16)


def shard_levels(own_key, extent, cuts, least, largest):
    def one(dim, blocks):
        draws = jax.random.uniform(jax.random.fold_in(jax.random.fold_in(own_key, 6), dim), (blocks,), jnp.float32, least / len(cuts), largest / len(cuts))
        return jnp.repeat(jnp.exp(draws), extent[dim] // blocks).reshape((-1,) + (1,) * (len(extent) - dim - 1))

    gain = one(*cuts[0])
    for cut in cuts[1:]:
        gain = gain * one(*cut)
    return gain


def scatter_about(stream_key, extent, width, limit, pieces=(), kind=jnp.bfloat16):
    loudness = shard_levels(stream_key, extent, pieces, -0.22, 0.18) if pieces else 1.0
    values = jax.random.normal(stream_key, extent, jnp.float32) * width * loudness
    return jnp.minimum(jnp.maximum(values, -limit), limit).astype(kind)


def setup_inputs(seed: int = 0) -> dict:
    arg_keys = jax.random.split(jax.random.key(seed), 3)
    weights = draw_weights(jax.random.fold_in(arg_keys[2], 71), 0)
    factor_init = scatter_about(arg_keys[1], (GROUPS, R, D), 1.0, 6.0, ((0, 8),), jnp.float32)
    return dict(weights=weights, factor_init=factor_init)


gossip_rate = 0.5

def reference(weights, factor_init):
    groups = weights.shape[0]
    indices = jnp.arange(groups, dtype=jnp.int32)
    factor = factor_init
    basis = None
    for repeat in range(STEPS):
        factor_bf = factor.astype(jnp.bfloat16)

        def forward(index):
            here = weights[index]
            there = weights[(index + 1) % groups]
            start = factor_bf[index]
            first = lax.dot_general(start.astype(jnp.float32), here.astype(jnp.float32), (((1,), (1,)), ((), ())), preferred_element_type=jnp.float32)
            second = lax.dot_general(start.astype(jnp.float32), there.astype(jnp.float32), (((1,), (1,)), ((), ())), preferred_element_type=jnp.float32)
            return first - second
        raw = lax.map(forward, indices)
        gram = jnp.einsum('grf,gsf->grs', raw, raw, precision=lax.Precision.HIGHEST)
        lower = lax.linalg.cholesky(gram)
        basis = lax.linalg.triangular_solve(lower, raw, left_side=True, lower=True)
        basis_bf = basis.astype(jnp.bfloat16)

        def backward(index):
            here = weights[index]
            there = weights[(index + 1) % groups]
            rows = basis_bf[index]
            return jnp.dot(rows.astype(jnp.float32), here.astype(jnp.float32), preferred_element_type=jnp.float32) - jnp.dot(rows.astype(jnp.float32), there.astype(jnp.float32), preferred_element_type=jnp.float32)
        factor = lax.map(backward, indices)

    def update(index):
        before = (index + groups - 1) % groups
        signed = jnp.concatenate([-basis[before], basis[index]], axis=0)
        factors = jnp.concatenate([factor[before], factor[index]], axis=0)
        delta = lax.dot_general(signed.astype(jnp.float32), factors.astype(jnp.float32), (((0,), (0,)), ((), ())), precision=lax.Precision.HIGHEST, preferred_element_type=jnp.float32)
        return (weights[index].astype(jnp.float32) - gossip_rate * delta).astype(jnp.bfloat16)
    new_weights = lax.map(update, indices)
    return (new_weights, factor)
```

```python
import functools

import jax
import jax.numpy as jnp
from jax import lax
from jax.experimental import pallas as pl
from jax.experimental.pallas import tpu as pltpu
from jax.sharding import PartitionSpec as P

STEPS = 2
RANK = 16
gossip_rate = 0.5

BF = jnp.bfloat16
F32 = jnp.float32
MESH = pl.DeviceIdType.MESH

ZS = 8
BLOCK = 896
PAD = 1024
HALF = 512
PIECE = 256
HIDDEN = 320
WIDE = 384

ORDER = (4, 3, 5, 2, 6, 1, 7, 0)
PEERS = tuple((d, e) for d in ORDER for e in (1, 0) if d or e)


def split3(x):
    hi = x.astype(BF)
    rest = x - hi.astype(F32)
    mid = rest.astype(BF)
    lo = (rest - mid.astype(F32)).astype(BF)
    return hi, mid, lo


def inverse_factors(gram):
    both = jnp.stack([gram, pltpu.roll(gram, 128 - RANK, axis=1)])
    row = lax.broadcasted_iota(jnp.int32, (2, RANK, 128), 1)
    lane = lax.broadcasted_iota(jnp.int32, (2, RANK, 128), 2)
    eye = jnp.where(lane - RANK == row, 1.0, 0.0)
    a = jnp.where(lane < RANK, both, eye)
    for k in range(RANK - 1):
        pivot = a[:, k : k + 1, :]
        m = jnp.where(row[:, :, :1] > k, a[:, :, k : k + 1] / pivot[:, :, k : k + 1], 0.0)
        a = a - m * pivot
    diagonal = jnp.sum(jnp.where(lane == row, a, 0.0), axis=2, keepdims=True)
    return a / jnp.sqrt(diagonal)


def apply_lower(inverse, x):
    total = inverse[:, RANK : RANK + 1] * x[0:1, :]
    for k in range(1, RANK):
        total = total + inverse[:, RANK + k : RANK + k + 1] * x[k : k + 1, :]
    return total


def main_kernel(
    w_hbm, f0_ref, basis_ref, fac_ref,
    w, f, xs, xr, gs, gc, gz, p, q, sb, t, dd, r, y,
    w_sem, init_s, init_r, x_s, x_r, gc_s, gc_r, gz_s, gz_r,
    q_s, q_r, t_s, t_r, r_s, r_r, az_s, az_r, ag_s, ag_r, ac_s, ac_r,
):
    g = lax.axis_index("group")
    s = lax.axis_index("shard")
    z, xh, c = s // 4, (s // 2) % 2, s % 2
    other = (g, s + 1 - 2 * c)
    left, right = ((g + 7) % 8, s), ((g + 1) % 8, s)
    across = ((g + 7 + 2 * c) % 8, s + 1 - 2 * c)
    mine = 1 - c

    def peer(d, e):
        return (g, ((z + d) % ZS) * 4 + ((xh + e) % 2) * 2 + c)

    started = []

    def send(src, dst, ss, rs, to):
        copy = pltpu.make_async_remote_copy(
            src_ref=src, dst_ref=dst, send_sem=ss, recv_sem=rs, device_id=to, device_id_type=MESH
        )
        copy.start()
        started.append(copy)
        return copy

    loads = []
    for b in range(ZS):
        load = pltpu.make_async_copy(w_hbm.at[:, pl.ds(b * BLOCK, BLOCK)], w.at[b], w_sem.at[b])
        load.start()
        loads.append(load)

    barrier = pltpu.get_barrier_semaphore()
    greeted = [other, left, right, across] + [peer(d, e) for d, e in PEERS]
    for device in greeted:
        pl.semaphore_signal(barrier, inc=1, device_id=device, device_id_type=MESH)

    for b in range(ZS):
        f[0, 1, b, :, :BLOCK] = f0_ref[:, b * BLOCK : (b + 1) * BLOCK].astype(BF)
    pl.semaphore_wait(barrier, len(greeted))

    here = pl.ds(pl.multiple_of(c * HALF, HALF), HALF)
    there = pl.ds(pl.multiple_of((1 - c) * HALF, HALF), HALF)
    first = send(f.at[0, 1, :, :, here], f.at[0, 0, :, :, here], init_s.at[0], init_r.at[0], right)
    for load in loads:
        load.wait()
    first.wait_recv()
    second = send(f.at[0, 0, :, :, here], f.at[0, 0, :, :, here], init_s.at[1], init_r.at[1], other)
    second.wait_recv()

    for step in range(STEPS):
        own = jnp.zeros((2 * RANK, HIDDEN), F32)
        for b in range(ZS):
            lhs = f[step, :, b, :, :BLOCK].reshape(2 * RANK, BLOCK)
            own = own + lax.dot_general(
                lhs, w[b], (((1,), (1,)), ((), ())), preferred_element_type=F32
            )
        own = jnp.concatenate([own, jnp.zeros((2 * RANK, WIDE - HIDDEN), F32)], axis=1)
        xs[step, 0] = own[:RANK]
        xs[step, 1] = own[RANK:]
        to_right = send(xs.at[step, 1], xr.at[step, 0], x_s.at[step, 1], x_r.at[step, 0], right)
        to_left = send(xs.at[step, 0], xr.at[step, 1], x_s.at[step, 0], x_r.at[step, 1], left)
        to_right.wait_recv()
        to_left.wait_recv()
        raw = jnp.concatenate([xr[step, 0] - own[:RANK], own[RANK:] - xr[step, 1]], axis=0)

        square = lax.dot_general(
            raw, raw, (((1,), (1,)), ((), ())),
            precision=lax.Precision.HIGHEST, preferred_element_type=F32,
        )
        square = jnp.concatenate([square, jnp.zeros((2 * RANK, 128 - 2 * RANK), F32)], axis=1)
        lane = lax.broadcasted_iota(jnp.int32, (RANK, 128), 1)
        gram = jnp.where(lane < RANK, square[:RANK], square[RANK:])
        gs[step, 0] = gram
        gram_core = send(gs.at[step, 0], gc.at[step], gc_s.at[step], gc_r.at[step], other)

        stacked = jnp.concatenate(split3(raw), axis=0)[:, :HIDDEN]
        core_copies = []
        for i, d in enumerate(ORDER):
            b = (z + d) % ZS
            prod = jnp.dot(stacked, w[b], preferred_element_type=F32)
            prod = prod[: 2 * RANK] + (prod[2 * RANK : 4 * RANK] + prod[4 * RANK :])
            p[step, 0, i, :, :BLOCK] = prod[:RANK]
            p[step, 1, i, :, :BLOCK] = prod[RANK:]
            core_copies.append(send(
                p.at[step, 1 - c, i, :, pl.ds(0, BLOCK)], q.at[step, i, :, pl.ds(0, BLOCK)],
                q_s.at[step, i], q_r.at[step, i], other,
            ))

        gram_core.wait_recv()
        gram = gram + gc[step]
        gs[step, 1] = gram
        gram_copies = [
            send(gs.at[step, 1], gz.at[step, j], gz_s.at[step, j], gz_r.at[step, j], peer(d, e))
            for j, (d, e) in enumerate(PEERS)
        ]

        cross_copies = []
        for i in range(ZS):
            core_copies[i].wait_recv()
            sb[step, i] = p[step, c, i] + q[step, i]
            cross_copies.append(send(
                sb.at[step, i, :, here], t.at[step, i], t_s.at[step, i], t_r.at[step, i], across
            ))

        sign = (2 * c - 1).astype(F32)
        reduce_copies = []
        for i, d in enumerate(ORDER):
            cross_copies[i].wait_recv()
            dd[step, i] = sign * (sb[step, i, :, there] - t[step, i])
            for e in (1, 0):
                if d or e:
                    j = len(reduce_copies)
                    part = pl.ds(pl.multiple_of(((xh + e) % 2) * PIECE, PIECE), PIECE)
                    reduce_copies.append(send(
                        dd.at[step, i, :, part], r.at[step, j],
                        r_s.at[step, j], r_r.at[step, j], peer(d, e),
                    ))

        for j, copy in enumerate(gram_copies):
            copy.wait_recv()
            gram = gram + gz[step, j]
        inverses = inverse_factors(gram)
        inverse = jnp.where(c == 0, inverses[0], inverses[1])

        own_part = pl.ds(pl.multiple_of(xh * PIECE, PIECE), PIECE)
        total = dd[step, ZS - 1, :, own_part]
        for j, copy in enumerate(reduce_copies):
            copy.wait_recv()
            total = total + r[step, j]
        piece = apply_lower(inverse, total).astype(BF)

        slot = pl.ds(pl.multiple_of(mine * HALF + xh * PIECE, PIECE), PIECE)
        y[step] = piece
        f[step + 1, c, z, :, slot] = piece
        gathers = [
            send(y.at[step], f.at[step + 1, c, z, :, slot], az_s.at[step, j], az_r.at[step, j], peer(d, e))
            for j, (d, e) in enumerate(PEERS)
        ]
        if step == STEPS - 1:
            basis_ref[:RANK] = -apply_lower(inverses[0], raw[:RANK])
            basis_ref[RANK:] = apply_lower(inverses[1], raw[RANK:])
        for copy in gathers:
            copy.wait_recv()
        half = f.at[step + 1, c, :, :, there]
        cross = send(half, f.at[step + 1, 1 - c, :, :, there], ag_s.at[step], ag_r.at[step], across)
        cross.wait_recv()
        last = send(f.at[step + 1, c], f.at[step + 1, c], ac_s.at[step], ac_r.at[step], other)
        last.wait_recv()

    fac_ref[...] = f[STEPS]
    for copy in started:
        copy.wait_send()


def update_kernel(w_ref, basis_ref, fac_ref, new_ref, next_ref, lhs):
    @pl.when(pl.program_id(0) == 0)
    def _():
        hi, mid, lo = split3(basis_ref[...] * gossip_rate)
        rows = jnp.concatenate([hi.astype(F32), mid.astype(F32), lo.astype(F32), jnp.zeros((2 * RANK, WIDE), F32)], axis=0)
        lhs[...] = rows.T.astype(BF)

    fac = fac_ref[:, 0, :, :BLOCK].reshape(2 * RANK, BLOCK)
    rhs = jnp.concatenate([fac, fac, fac, jnp.zeros_like(fac)], axis=0)
    delta = jnp.dot(lhs[:HIDDEN, :], rhs, preferred_element_type=F32)
    new_ref[0] = (w_ref[0].astype(F32) - delta).astype(BF)
    next_ref[0] = fac_ref[1, 0, :, :BLOCK].astype(F32)


def body(weights, factor_init):
    dma = pltpu.SemaphoreType.DMA
    n = len(PEERS)
    basis, fac = pl.pallas_call(
        main_kernel,
        name="rounds",
        out_shape=(
            jax.ShapeDtypeStruct((2 * RANK, WIDE), F32),
            jax.ShapeDtypeStruct((2, ZS, RANK, PAD), BF),
        ),
        in_specs=[pl.BlockSpec(memory_space=pl.ANY), pl.BlockSpec(memory_space=pltpu.VMEM)],
        out_specs=[pl.BlockSpec(memory_space=pltpu.VMEM)] * 2,
        scratch_shapes=[
            pltpu.VMEM((ZS, HIDDEN, BLOCK), BF),
            pltpu.VMEM((STEPS + 1, 2, ZS, RANK, PAD), BF),
            pltpu.VMEM((STEPS, 2, RANK, WIDE), F32),
            pltpu.VMEM((STEPS, 2, RANK, WIDE), F32),
            pltpu.VMEM((STEPS, 2, RANK, 128), F32),
            pltpu.VMEM((STEPS, RANK, 128), F32),
            pltpu.VMEM((STEPS, n, RANK, 128), F32),
            pltpu.VMEM((STEPS, 2, ZS, RANK, PAD), F32),
            pltpu.VMEM((STEPS, ZS, RANK, PAD), F32),
            pltpu.VMEM((STEPS, ZS, RANK, PAD), F32),
            pltpu.VMEM((STEPS, ZS, RANK, HALF), F32),
            pltpu.VMEM((STEPS, ZS, RANK, HALF), F32),
            pltpu.VMEM((STEPS, n, RANK, PIECE), F32),
            pltpu.VMEM((STEPS, RANK, PIECE), BF),
            dma((ZS,)),
            dma((2,)), dma((2,)),
            dma((STEPS, 2)), dma((STEPS, 2)),
            dma((STEPS,)), dma((STEPS,)),
            dma((STEPS, n)), dma((STEPS, n)),
            dma((STEPS, ZS)), dma((STEPS, ZS)),
            dma((STEPS, ZS)), dma((STEPS, ZS)),
            dma((STEPS, n)), dma((STEPS, n)),
            dma((STEPS, n)), dma((STEPS, n)),
            dma((STEPS,)), dma((STEPS,)),
            dma((STEPS,)), dma((STEPS,)),
        ],
        compiler_params=pltpu.CompilerParams(
            collective_id=0, has_side_effects=True, vmem_limit_bytes=48 * 2**20
        ),
        cost_estimate=pl.CostEstimate(
            flops=10 * 32 * HIDDEN * 7168, bytes_accessed=HIDDEN * 7168 * 2, transcendentals=0
        ),
    )(weights[0], factor_init[0])
    new, nxt = pl.pallas_call(
        update_kernel,
        name="update",
        grid=(ZS,),
        out_shape=(
            jax.ShapeDtypeStruct(weights.shape, BF),
            jax.ShapeDtypeStruct(factor_init.shape, F32),
        ),
        in_specs=[
            pl.BlockSpec((1, HIDDEN, BLOCK), lambda b: (0, 0, b)),
            pl.BlockSpec((2 * RANK, WIDE), lambda b: (0, 0)),
            pl.BlockSpec((2, 1, RANK, PAD), lambda b: (0, b, 0, 0)),
        ],
        out_specs=[
            pl.BlockSpec((1, HIDDEN, BLOCK), lambda b: (0, 0, b)),
            pl.BlockSpec((1, RANK, BLOCK), lambda b: (0, 0, b)),
        ],
        scratch_shapes=[pltpu.VMEM((WIDE, 128), BF)],
        compiler_params=pltpu.CompilerParams(vmem_limit_bytes=32 * 2**20),
        cost_estimate=pl.CostEstimate(
            flops=2 * 128 * HIDDEN * 7168, bytes_accessed=HIDDEN * 7168 * 4, transcendentals=0
        ),
    )(weights, basis, fac)
    return new, nxt


def solution(mesh):
    in_specs = (P("group", "shard", None), P("group", None, None))
    out_specs = (P("group", "shard", None), P("group", None, None))
    return jax.shard_map(body, mesh=mesh, in_specs=in_specs, out_specs=out_specs, check_vma=False)
```

```python
import functools

import jax
import jax.numpy as jnp
from jax import lax
from jax.experimental import pallas as pl
from jax.experimental.pallas import tpu as pltpu
from jax.sharding import PartitionSpec as P

STEPS = 2
RANK = 16
gossip_rate = 0.5

BF = jnp.bfloat16
F32 = jnp.float32
MESH = pl.DeviceIdType.MESH

ZS = 8
BLOCK = 896
SKEW = 384
PART = 512
TILE = 128
HIDDEN = 320
BOTH = 640

ORDER = (4, 3, 5, 2, 6, 1, 7, 0)
GRAM_AT = 1
PEERS = tuple((d, e) for d in ORDER for e in (1, 0) if d or e)


def split3(x):
    hi = x.astype(BF)
    rest = x - hi.astype(F32)
    mid = rest.astype(BF)
    lo = (rest - mid.astype(F32)).astype(BF)
    return hi, mid, lo


def inverse_factors(gram):
    both = jnp.stack([gram, pltpu.roll(gram, 128 - RANK, axis=1)])
    row = lax.broadcasted_iota(jnp.int32, (2, RANK, 128), 1)
    lane = lax.broadcasted_iota(jnp.int32, (2, RANK, 128), 2)
    eye = jnp.where(lane - RANK == row, 1.0, 0.0)
    a = jnp.where(lane < RANK, both, eye)
    for k in range(RANK - 1):
        pivot = a[:, k : k + 1, :]
        m = jnp.where(row[:, :, :1] > k, a[:, :, k : k + 1] / pivot[:, :, k : k + 1], 0.0)
        a = a - m * pivot
    diagonal = jnp.sum(jnp.where(lane == row, a, 0.0), axis=2, keepdims=True)
    return a / jnp.sqrt(diagonal)


def apply_lower(inverse, x):
    total = inverse[:, RANK : RANK + 1] * x[0:1, :]
    for k in range(1, RANK):
        total = total + inverse[:, RANK + k : RANK + k + 1] * x[k : k + 1, :]
    return total


def main_kernel(
    w_hbm, f0_hbm, lhs_ref, fac_ref,
    w, f0, f, xs, xc, xo, xr, gs, gz, pk, ps, pr, dd, r, fo, bt,
    w_sem, f0_sem, wx_s, wx_r, init_s, init_r, c_s, c_r, x_s, x_r, gz_s, gz_r,
    p_s, p_r, r_s, r_r, az_s, az_r, ag_s, ag_r, ac_s, ac_r,
):
    g = lax.axis_index("group")
    s = lax.axis_index("shard")
    z, xh, c = s // 4, (s // 2) % 2, s % 2
    other = (g, s + 1 - 2 * c)
    left, right = ((g + 7) % 8, s), ((g + 1) % 8, s)

    def peer(d, e):
        return (g, ((z + d) % ZS) * 4 + ((xh + e) % 2) * 2 + c)

    started = []

    def send(src, dst, ss, rs, to):
        copy = pltpu.make_async_remote_copy(
            src_ref=src, dst_ref=dst, send_sem=ss, recv_sem=rs, device_id=to, device_id_type=MESH
        )
        copy.start()
        started.append(copy)
        return copy

    def columns(b, core):
        return pl.ds(pl.multiple_of(b * BLOCK + core * SKEW, TILE), PART)

    f0_load = pltpu.make_async_copy(f0_hbm, f0, f0_sem)
    f0_load.start()
    loads = []
    for b in range(ZS):
        load = pltpu.make_async_copy(w_hbm.at[:, columns(b, c)], w.at[b, c], w_sem.at[b])
        load.start()
        loads.append(load)

    barrier = pltpu.get_barrier_semaphore()
    greeted = [other, left, right] + [peer(d, e) for d, e in PEERS]
    for device in greeted:
        pl.semaphore_signal(barrier, inc=1, device_id=device, device_id_type=MESH)

    f0_load.wait()
    for b in range(ZS):
        for t in range(4):
            tile = pl.ds(pl.multiple_of(b * BLOCK + c * SKEW + t * TILE, TILE), TILE)
            f[0, t // 2, b, t % 2, 1] = f0[:, tile].astype(BF)
    pl.semaphore_wait(barrier, len(greeted))

    arrive = [
        send(f.at[0, kind, :, :, 1], f.at[0, 1 - kind, :, :, 0], init_s.at[kind], init_r.at[kind], right)
        for kind in range(2)
    ]
    for b in range(ZS):
        arrive.append(send(w_hbm.at[:, columns(b, 1 - c)], w.at[b, c], wx_s.at[b], wx_r.at[b], other))
    for load in loads:
        load.wait()
    for copy in arrive:
        copy.wait_recv()

    for step in range(STEPS):
        part = jnp.zeros((2 * RANK, BOTH), F32)
        for b in range(ZS):
            tiles = []
            for t in range(4):
                k = t // 2
                tile = jnp.concatenate([f[step, 1 - k, b, t % 2, 0], f[step, k, b, t % 2, 1]], axis=0)
                if t == 0:
                    tile = jnp.where(c == 1, jnp.zeros_like(tile), tile)
                tiles.append(tile)
            part = part + lax.dot_general(
                jnp.concatenate(tiles, axis=1), w[b].reshape(BOTH, PART),
                (((1,), (1,)), ((), ())), preferred_element_type=F32,
            )
        xs[step, 0] = part[:RANK]
        xs[step, 1] = part[RANK:]
        core_copy = send(xs.at[step], xc.at[step], c_s.at[step], c_r.at[step], other)
        core_copy.wait_recv()
        own_left = part[:RANK] + xc[step, 0]
        own_right = part[RANK:] + xc[step, 1]
        xo[step, 0] = own_left
        xo[step, 1] = own_right
        to_right = send(xo.at[step, 1], xr.at[step, 0], x_s.at[step, 1], x_r.at[step, 0], right)
        to_left = send(xo.at[step, 0], xr.at[step, 1], x_s.at[step, 0], x_r.at[step, 1], left)
        to_right.wait_recv()
        to_left.wait_recv()
        raw = jnp.concatenate([xr[step, 0] - own_left, own_right - xr[step, 1]], axis=0)

        stacked = jnp.concatenate(split3(raw), axis=0)
        cross_copies = []
        for i, d in enumerate(ORDER):
            b = (z + d) % ZS
            prod = jnp.dot(stacked, w[b].reshape(BOTH, PART), preferred_element_type=F32)
            prod = prod[: 2 * RANK] + (prod[2 * RANK : 4 * RANK] + prod[4 * RANK :])
            half = PART // 2
            ps[step, i, 0] = prod[:RANK, :half]
            ps[step, i, 1] = prod[RANK:, half:]
            pk[step, i, 0] = prod[:RANK, half:]
            pk[step, i, 1] = prod[RANK:, :half]
            cross_copies.append((
                send(ps.at[step, i, 1], pr.at[step, i, 0], p_s.at[step, i, 1], p_r.at[step, i, 0], right),
                send(ps.at[step, i, 0], pr.at[step, i, 1], p_s.at[step, i, 0], p_r.at[step, i, 1], left),
            ))
            if i == GRAM_AT:
                square = lax.dot_general(
                    raw, raw, (((1,), (1,)), ((), ())),
                    precision=lax.Precision.HIGHEST, preferred_element_type=F32,
                )
                square = jnp.concatenate([square, jnp.zeros((2 * RANK, TILE - 2 * RANK), F32)], axis=1)
                lane = lax.broadcasted_iota(jnp.int32, (RANK, TILE), 1)
                gram = jnp.where(lane < RANK, square[:RANK], square[RANK:])
                gs[step] = gram
                gram_copies = [
                    send(gs.at[step], gz.at[step, j], gz_s.at[step, j], gz_r.at[step, j], peer(d2, e2))
                    for j, (d2, e2) in enumerate(PEERS)
                ]

        reduce_copies = []
        for i, d in enumerate(ORDER):
            for copy in cross_copies[i]:
                copy.wait_recv()
            diff_left = pr[step, i, 0] - pk[step, i, 0]
            diff_right = pk[step, i, 1] - pr[step, i, 1]
            for t in range(2):
                dd[step, i, t, 0] = diff_left[:, t * TILE : (t + 1) * TILE]
                dd[step, i, t, 1] = diff_right[:, t * TILE : (t + 1) * TILE]
            for e in (1, 0):
                if d or e:
                    j = len(reduce_copies)
                    reduce_copies.append(send(
                        dd.at[step, i, (xh + e) % 2], r.at[step, j],
                        r_s.at[step, j], r_r.at[step, j], peer(d, e),
                    ))

        for j, copy in enumerate(gram_copies):
            copy.wait_recv()
            gram = gram + gz[step, j]
        inverses = inverse_factors(gram)

        total = dd[step, ZS - 1, xh]
        for j, copy in enumerate(reduce_copies):
            copy.wait_recv()
            total = total + r[step, j]

        f[step + 1, 0, z, xh, 0] = apply_lower(inverses[0], total[0]).astype(BF)
        f[step + 1, 0, z, xh, 1] = apply_lower(inverses[1], total[1]).astype(BF)
        piece = f.at[step + 1, 0, z, xh]
        gathers = [
            send(piece, piece, az_s.at[step, j], az_r.at[step, j], peer(d, e))
            for j, (d, e) in enumerate(PEERS)
        ]
        if step == STEPS - 1:
            basis = gossip_rate * jnp.concatenate(
                [-apply_lower(inverses[0], raw[:RANK]), apply_lower(inverses[1], raw[RANK:])], axis=0
            )
            terms = [term.astype(F32) for term in split3(basis)]
            bt[...] = jnp.concatenate(terms + [jnp.zeros((2 * RANK, BOTH), F32)], axis=0).T
            lhs_ref[...] = bt[pl.ds(pl.multiple_of(c * HIDDEN, 16), HIDDEN), :].astype(BF)
        for copy in gathers:
            copy.wait_recv()
        to_right = send(
            f.at[step + 1, 0, :, :, 1], f.at[step + 1, 1, :, :, 0], ag_s.at[step, 1], ag_r.at[step, 0], right
        )
        to_left = send(
            f.at[step + 1, 0, :, :, 0], f.at[step + 1, 1, :, :, 1], ag_s.at[step, 0], ag_r.at[step, 1], left
        )
        to_right.wait_recv()
        to_left.wait_recv()

    last = send(f.at[STEPS], fo, ac_s, ac_r, other)
    fac_ref[c] = f[STEPS]
    last.wait_recv()
    fac_ref[1 - c] = fo[...]
    for copy in started:
        copy.wait_send()


def update_kernel(w_ref, lhs_ref, fac_ref, new_ref, next_ref):
    tiles = []
    for core in range(2):
        for t in range(core, 4):
            k = t // 2
            tiles.append(jnp.concatenate(
                [fac_ref[core, 1 - k, 0, t % 2, 0], fac_ref[core, k, 0, t % 2, 1]], axis=0
            ))
    fac = jnp.concatenate(tiles, axis=1)
    rhs = jnp.concatenate([fac, fac, fac, jnp.zeros_like(fac)], axis=0)
    delta = jnp.dot(lhs_ref[...], rhs, preferred_element_type=F32)
    new_ref[0] = (w_ref[0].astype(F32) - delta).astype(BF)
    next_ref[0] = fac[RANK:].astype(F32)


def body(weights, factor_init):
    dma = pltpu.SemaphoreType.DMA
    n = len(PEERS)
    lhs, fac = pl.pallas_call(
        main_kernel,
        name="rounds",
        out_shape=(
            jax.ShapeDtypeStruct((HIDDEN, TILE), BF),
            jax.ShapeDtypeStruct((2, 2, ZS, 2, 2, RANK, TILE), BF),
        ),
        in_specs=[pl.BlockSpec(memory_space=pl.ANY)] * 2,
        out_specs=[pl.BlockSpec(memory_space=pltpu.VMEM)] * 2,
        scratch_shapes=[
            pltpu.VMEM((ZS, 2, HIDDEN, PART), BF),
            pltpu.VMEM((RANK, ZS * BLOCK), F32),
            pltpu.VMEM((STEPS + 1, 2, ZS, 2, 2, RANK, TILE), BF),
            pltpu.VMEM((STEPS, 2, RANK, BOTH), F32),
            pltpu.VMEM((STEPS, 2, RANK, BOTH), F32),
            pltpu.VMEM((STEPS, 2, RANK, BOTH), F32),
            pltpu.VMEM((STEPS, 2, RANK, BOTH), F32),
            pltpu.VMEM((STEPS, RANK, TILE), F32),
            pltpu.VMEM((STEPS, n, RANK, TILE), F32),
            pltpu.VMEM((STEPS, ZS, 2, RANK, PART // 2), F32),
            pltpu.VMEM((STEPS, ZS, 2, RANK, PART // 2), F32),
            pltpu.VMEM((STEPS, ZS, 2, RANK, PART // 2), F32),
            pltpu.VMEM((STEPS, ZS, 2, 2, RANK, TILE), F32),
            pltpu.VMEM((STEPS, n, 2, RANK, TILE), F32),
            pltpu.VMEM((2, ZS, 2, 2, RANK, TILE), BF),
            pltpu.VMEM((BOTH, TILE), F32),
            dma((ZS,)), dma(()),
            dma((ZS,)), dma((ZS,)),
            dma((2,)), dma((2,)),
            dma((STEPS,)), dma((STEPS,)),
            dma((STEPS, 2)), dma((STEPS, 2)),
            dma((STEPS, n)), dma((STEPS, n)),
            dma((STEPS, ZS, 2)), dma((STEPS, ZS, 2)),
            dma((STEPS, n)), dma((STEPS, n)),
            dma((STEPS, n)), dma((STEPS, n)),
            dma((STEPS, 2)), dma((STEPS, 2)),
            dma(()), dma(()),
        ],
        compiler_params=pltpu.CompilerParams(
            collective_id=0, has_side_effects=True, vmem_limit_bytes=60 * 2**20
        ),
        cost_estimate=pl.CostEstimate(
            flops=10 * 32 * HIDDEN * 7168, bytes_accessed=HIDDEN * 7168 * 2, transcendentals=0
        ),
    )(weights[0], factor_init[0])
    new, nxt = pl.pallas_call(
        update_kernel,
        name="update",
        grid=(ZS,),
        out_shape=(
            jax.ShapeDtypeStruct(weights.shape, BF),
            jax.ShapeDtypeStruct(factor_init.shape, F32),
        ),
        in_specs=[
            pl.BlockSpec((1, HIDDEN, BLOCK), lambda b: (0, 0, b)),
            pl.BlockSpec((HIDDEN, TILE), lambda b: (0, 0)),
            pl.BlockSpec((2, 2, 1, 2, 2, RANK, TILE), lambda b: (0, 0, b, 0, 0, 0, 0)),
        ],
        out_specs=[
            pl.BlockSpec((1, HIDDEN, BLOCK), lambda b: (0, 0, b)),
            pl.BlockSpec((1, RANK, BLOCK), lambda b: (0, 0, b)),
        ],
        compiler_params=pltpu.CompilerParams(vmem_limit_bytes=32 * 2**20),
        cost_estimate=pl.CostEstimate(
            flops=2 * 128 * HIDDEN * 7168, bytes_accessed=HIDDEN * 7168 * 4, transcendentals=0
        ),
    )(weights, lhs, fac)
    return new, nxt


def solution(mesh):
    in_specs = (P("group", "shard", None), P("group", None, None))
    out_specs = (P("group", "shard", None), P("group", None, None))
    return jax.shard_map(body, mesh=mesh, in_specs=in_specs, out_specs=out_specs, check_vma=False)
```

```python
import functools

import jax
import jax.numpy as jnp
from jax import lax
from jax.experimental import pallas as pl
from jax.experimental.pallas import tpu as pltpu
from jax.sharding import PartitionSpec as P

STEPS = 2
RANK = 16
gossip_rate = 0.5

BF = jnp.bfloat16
F32 = jnp.float32
MESH = pl.DeviceIdType.MESH

ZS = 8
BLOCK = 896
SKEW = 384
PART = 512
TILE = 128
HIDDEN = 320
BOTH = 640

ORDER = (4, 3, 5, 2, 6, 1, 7, 0)
NEAR = (0, 1, 7, 2, 6, 3, 5, 4)
GRAM_AT = 1
GRAM_ON = 2
ALL = tuple((d, e) for d in ORDER for e in (1, 0))
PEERS = tuple((d, e) for d in ORDER for e in (1, 0) if d or e)


def split3(x):
    hi = x.astype(BF)
    rest = x - hi.astype(F32)
    mid = rest.astype(BF)
    lo = (rest - mid.astype(F32)).astype(BF)
    return hi, mid, lo


def pack_gram(square):
    wide = jnp.concatenate([square, jnp.zeros((2 * RANK, TILE - 2 * RANK), F32)], axis=1)
    lane = lax.broadcasted_iota(jnp.int32, (8, TILE), 1)
    packed = jnp.where(lane < RANK, wide[:8], pltpu.roll(wide[8:16], RANK, axis=1))
    packed = jnp.where(lane < 2 * RANK, packed, pltpu.roll(wide[16:24], RANK, axis=1))
    return jnp.where(lane < 3 * RANK, packed, pltpu.roll(wide[24:], 2 * RANK, axis=1))


def inverse_factors(packed):
    rolled = [packed] + [pltpu.roll(packed, TILE - k * RANK, axis=1) for k in range(1, 4)]
    both = jnp.concatenate(rolled, axis=0).reshape(2, RANK, TILE)
    row = lax.broadcasted_iota(jnp.int32, (2, RANK, TILE), 1)
    lane = lax.broadcasted_iota(jnp.int32, (2, RANK, TILE), 2)
    eye = jnp.where(lane - RANK == row, 1.0, 0.0)
    a = jnp.where(lane < RANK, both, eye)
    for k in range(RANK - 1):
        pivot = a[:, k : k + 1, :]
        m = jnp.where(row[:, :, :1] > k, a[:, :, k : k + 1] / pivot[:, :, k : k + 1], 0.0)
        a = a - m * pivot
    diagonal = jnp.sum(jnp.where(lane == row, a, 0.0), axis=2, keepdims=True)
    return a / jnp.sqrt(diagonal)


def apply_lower(inverse, x):
    total = inverse[:, RANK : RANK + 1] * x[0:1, :]
    for k in range(1, RANK):
        total = total + inverse[:, RANK + k : RANK + k + 1] * x[k : k + 1, :]
    return total


def main_kernel(
    w_hbm, f0, lhs_ref, fac_ref,
    w, f, xs, xc, xr, gs, gx, gz, pk, ps, pr, dd, r, bt,
    hop, w_sem, wx_s, wx_r, init_s, init_r, c_s, c_r, x_s, x_r, gx_s, gx_r, gz_s, gz_r,
    p_s, p_r, r_s, r_r, az_s, az_r, ag_s, ag_r, ac_s, ac_r,
):
    g = lax.axis_index("group")
    s = lax.axis_index("shard")
    z, xh, c = s // 4, (s // 2) % 2, s % 2
    other = (g, s + 1 - 2 * c)
    left, right = ((g + 7) % 8, s), ((g + 1) % 8, s)

    def peer(d, e):
        return (g, ((z + d) % ZS) * 4 + ((xh + e) % 2) * 2 + c)

    started = []

    def send(src, dst, ss, rs, to):
        copy = pltpu.make_async_remote_copy(
            src_ref=src, dst_ref=dst, send_sem=ss, recv_sem=rs, device_id=to, device_id_type=MESH
        )
        copy.start()
        started.append(copy)
        return copy

    def columns(b, core):
        return pl.ds(pl.multiple_of(b * BLOCK + core * SKEW, TILE), PART)

    beyond = [((g + k) % 8, s + 1 - 2 * c) for k in (7, 1)]
    barrier = pltpu.get_barrier_semaphore()
    above, below = peer(1, 0), peer(7, 0)
    aside = [((g + k) % 8, peer(0, 1)[1]) for k in (7, 1)]
    greeted = [other, left, right, above, below, peer(0, 1)] + beyond + aside
    for device in greeted:
        pl.semaphore_signal(barrier, inc=1, device_id=device, device_id_type=MESH)

    loads = []
    for b in range(ZS):
        load = pltpu.make_async_copy(w_hbm.at[:, columns(b, c)], w.at[b, c], w_sem.at[b])
        load.start()
        loads.append(load)

    for b in range(ZS):
        for t in range(4):
            tile = pl.ds(pl.multiple_of(b * BLOCK + c * SKEW + t * TILE, TILE), TILE)
            f[0, b, t // 2, t % 2, 1] = f0[:, tile].astype(BF)
    pl.semaphore_wait(barrier, len(greeted))

    first, swaps = [], []
    for b in range(ZS):
        if b % 2 == 0:
            two = pl.ds(b, 2)
            first.append([
                send(
                    f.at[0, two, k, :, 1], f.at[0, two, 1 - k, :, 0],
                    init_s.at[b // 2, k], init_r.at[b // 2, 1 - k], right,
                )
                for k in range(2)
            ])
        swaps.append(send(w_hbm.at[:, columns(b, 1 - c)], w.at[b, c], wx_s.at[b], wx_r.at[b], other))

    def tell(k):
        for way, device in enumerate((above, below)):
            pl.semaphore_signal(hop.at[k, way], inc=1, device_id=device, device_id_type=MESH)

    def hear(k):
        for way in range(2):
            pl.semaphore_wait(hop.at[k, way], 1)

    tell(0)
    gathers = {}
    for step in range(STEPS):
        part = jnp.zeros((2 * RANK, BOTH), F32)
        for i, d in enumerate(NEAR):
            if step == 0:
                b = i
                if i == 4:
                    hear(0)
                    tell(1)
                loads[b].wait()
                swaps[b].wait_recv()
                if b % 2 == 0:
                    for copy in first[b // 2]:
                        copy.wait_recv()
            else:
                b = (z + ZS - d) % ZS
                for e in range(2):
                    for copy in gathers[d, e]:
                        copy.wait_recv()
            tiles = []
            for t in range(4):
                k = t // 2
                tile = jnp.concatenate([f[step, b, 1 - k, t % 2, 0], f[step, b, k, t % 2, 1]], axis=0)
                if t == 0:
                    tile = jnp.where(c == 1, jnp.zeros_like(tile), tile)
                tiles.append(tile)
            part = part + lax.dot_general(
                jnp.concatenate(tiles, axis=1), w[b].reshape(BOTH, PART),
                (((1,), (1,)), ((), ())), preferred_element_type=F32,
            )
        xs[step, 0] = part[:RANK]
        xs[step, 1] = part[RANK:]
        if step == 0:
            hear(1)
            tell(2)
        swapped = [
            send(xs.at[step, side], xr.at[step, far, 1 - side], x_s.at[step, far, side], x_r.at[step, far, 1 - side], to)
            for side, same in ((1, right), (0, left))
            for far, to in ((0, same), (1, beyond[side]))
        ]
        swapped.append(send(xs.at[step], xc.at[step], c_s.at[step], c_r.at[step], other))
        for copy in swapped:
            copy.wait_recv()
        raw = jnp.concatenate([
            (xr[step, 0, 0] + xr[step, 1, 0]) - (part[:RANK] + xc[step, 0]),
            (part[RANK:] + xc[step, 1]) - (xr[step, 0, 1] + xr[step, 1, 1]),
        ], axis=0)

        if step == 0:
            hear(2)
            tell(3)

        stacked = jnp.concatenate(split3(raw), axis=0)
        cross_copies = []
        for i, d in enumerate(ORDER):
            b = (z + d) % ZS
            prod = jnp.dot(stacked, w[b].reshape(BOTH, PART), preferred_element_type=F32)
            prod = prod[: 2 * RANK] + (prod[2 * RANK : 4 * RANK] + prod[4 * RANK :])
            half = PART // 2
            ps[step, i, 0] = prod[:RANK, :half]
            ps[step, i, 1] = prod[RANK:, half:]
            pk[step, i, 0] = prod[:RANK, half:]
            pk[step, i, 1] = prod[RANK:, :half]
            cross_copies.append((
                send(ps.at[step, i, 1], pr.at[step, i, 0], p_s.at[step, i, 1], p_r.at[step, i, 0], right),
                send(ps.at[step, i, 0], pr.at[step, i, 1], p_s.at[step, i, 0], p_r.at[step, i, 1], left),
            ))
            if i == GRAM_AT:
                square = lax.dot_general(
                    raw, raw, (((1,), (1,)), ((), ())),
                    precision=lax.Precision.HIGHEST, preferred_element_type=F32,
                )
                gram = pack_gram(square)
                gs[step, 0] = gram
                gram_x = send(gs.at[step, 0], gx.at[step], gx_s.at[step], gx_r.at[step], peer(0, 1))

        reduce_copies = []
        for i, d in enumerate(ORDER):
            if i == 0 and step == 0:
                hear(3)
            if i == GRAM_ON:
                gram_x.wait_recv()
                gram = gram + gx[step]
                gs[step, 1] = gram
                gram_copies = [
                    send(gs.at[step, 1], gz.at[step, j], gz_s.at[step, j], gz_r.at[step, j], peer(d2, 0))
                    for j, d2 in enumerate(ORDER[:-1])
                ]
            for copy in cross_copies[i]:
                copy.wait_recv()
            diff_left = pr[step, i, 0] - pk[step, i, 0]
            diff_right = pk[step, i, 1] - pr[step, i, 1]
            for t in range(2):
                dd[step, i, t, 0] = diff_left[:, t * TILE : (t + 1) * TILE]
                dd[step, i, t, 1] = diff_right[:, t * TILE : (t + 1) * TILE]
            for e in (1, 0):
                if d or e:
                    j = len(reduce_copies)
                    reduce_copies.append(send(
                        dd.at[step, i, (xh + e) % 2], r.at[step, j],
                        r_s.at[step, j], r_r.at[step, j], peer(d, e),
                    ))

        for j, copy in enumerate(gram_copies):
            copy.wait_recv()
            gram = gram + gz[step, j]
        inverses = inverse_factors(gram)

        total = dd[step, ZS - 1, xh]
        for j, copy in enumerate(reduce_copies):
            copy.wait_recv()
            total = total + r[step, j]

        f[step + 1, z, 0, xh, 0] = apply_lower(inverses[0], total[0]).astype(BF)
        f[step + 1, z, 0, xh, 1] = apply_lower(inverses[1], total[1]).astype(BF)
        piece = f.at[step + 1, z, 0, xh]
        gathers = {}
        for j, (d, e) in enumerate(ALL):
            shard = peer(d, e)[1]
            gathers[d, e] = [
                send(
                    piece.at[side], f.at[step + 1, z, 1, xh, 1 - side],
                    ag_s.at[step, j, side], ag_r.at[step, j, 1 - side], (group, shard),
                )
                for side, group in ((1, (g + 1) % 8), (0, (g + 7) % 8))
            ]
            if d or e:
                gathers[d, e].append(send(piece, piece, az_s.at[step, j], az_r.at[step, j], (g, shard)))
        if step == STEPS - 1:
            basis = gossip_rate * jnp.concatenate(
                [-apply_lower(inverses[0], raw[:RANK]), apply_lower(inverses[1], raw[RANK:])], axis=0
            )
            terms = [term.astype(F32) for term in split3(basis)]
            bt[...] = jnp.concatenate(terms + [jnp.zeros((2 * RANK, BOTH), F32)], axis=0).T
            lhs_ref[...] = bt[pl.ds(pl.multiple_of(c * HIDDEN, 16), HIDDEN), :].astype(BF)

    lasts = []
    for i, d in enumerate(NEAR):
        b = (z + ZS - d) % ZS
        for e in range(2):
            for copy in gathers[d, e]:
                copy.wait_recv()
        lasts.append(send(f.at[STEPS, b], fac_ref.at[c, b], ac_s.at[i], ac_r.at[i], other))
        fac_ref[c, b] = f[STEPS, b]
    for copy in lasts:
        copy.wait_recv()
    for copy in started:
        copy.wait_send()


def update_kernel(w_ref, lhs_ref, fac_ref, new_hbm, next_hbm, new, nxt, new_sem, next_sem):
    stores = []
    for b in range(ZS):
        tiles = []
        for core in range(2):
            for t in range(core, 4):
                k = t // 2
                tiles.append(jnp.concatenate(
                    [fac_ref[core, b, 1 - k, t % 2, 0], fac_ref[core, b, k, t % 2, 1]], axis=0
                ))
        fac = jnp.concatenate(tiles, axis=1)
        rhs = jnp.concatenate([fac, fac, fac, jnp.zeros_like(fac)], axis=0)
        delta = jnp.dot(lhs_ref[...], rhs, preferred_element_type=F32)
        columns = slice(b * BLOCK, (b + 1) * BLOCK)
        new[b] = (w_ref[0, :, columns].astype(F32) - delta).astype(BF)
        store = pltpu.make_async_copy(new.at[b], new_hbm.at[0, :, columns], new_sem.at[b])
        store.start()
        stores.append(store)
        nxt[:, columns] = fac[RANK:].astype(F32)
    store = pltpu.make_async_copy(nxt, next_hbm.at[0], next_sem)
    store.start()
    for copy in [*stores, store]:
        copy.wait()


def body(weights, factor_init):
    dma = pltpu.SemaphoreType.DMA
    n = len(PEERS)
    lhs, fac = pl.pallas_call(
        main_kernel,
        name="rounds",
        out_shape=(
            jax.ShapeDtypeStruct((HIDDEN, TILE), BF),
            jax.ShapeDtypeStruct((2, ZS, 2, 2, 2, RANK, TILE), BF),
        ),
        in_specs=[pl.BlockSpec(memory_space=pltpu.HBM), pl.BlockSpec(memory_space=pltpu.VMEM)],
        out_specs=[pl.BlockSpec(memory_space=pltpu.VMEM)] * 2,
        scratch_shapes=[
            pltpu.VMEM((ZS, 2, HIDDEN, PART), BF),
            pltpu.VMEM((STEPS + 1, ZS, 2, 2, 2, RANK, TILE), BF),
            pltpu.VMEM((STEPS, 2, RANK, BOTH), F32),
            pltpu.VMEM((STEPS, 2, RANK, BOTH), F32),
            pltpu.VMEM((STEPS, 2, 2, RANK, BOTH), F32),
            pltpu.VMEM((STEPS, 2, 8, TILE), F32),
            pltpu.VMEM((STEPS, 8, TILE), F32),
            pltpu.VMEM((STEPS, ZS - 1, 8, TILE), F32),
            pltpu.VMEM((STEPS, ZS, 2, RANK, PART // 2), F32),
            pltpu.VMEM((STEPS, ZS, 2, RANK, PART // 2), F32),
            pltpu.VMEM((STEPS, ZS, 2, RANK, PART // 2), F32),
            pltpu.VMEM((STEPS, ZS, 2, 2, RANK, TILE), F32),
            pltpu.VMEM((STEPS, n, 2, RANK, TILE), F32),
            pltpu.VMEM((BOTH, TILE), F32),
            pltpu.SemaphoreType.REGULAR((4, 2)),
            dma((ZS,)),
            dma((ZS,)), dma((ZS,)),
            dma((ZS // 2, 2)), dma((ZS // 2, 2)),
            dma((STEPS,)), dma((STEPS,)),
            dma((STEPS, 2, 2)), dma((STEPS, 2, 2)),
            dma((STEPS,)), dma((STEPS,)),
            dma((STEPS, ZS - 1)), dma((STEPS, ZS - 1)),
            dma((STEPS, ZS, 2)), dma((STEPS, ZS, 2)),
            dma((STEPS, n)), dma((STEPS, n)),
            dma((STEPS, n + 1)), dma((STEPS, n + 1)),
            dma((STEPS, n + 1, 2)), dma((STEPS, n + 1, 2)),
            dma((ZS,)), dma((ZS,)),
        ],
        compiler_params=pltpu.CompilerParams(
            collective_id=0, has_side_effects=True, vmem_limit_bytes=52 * 2**20
        ),
        cost_estimate=pl.CostEstimate(
            flops=10 * 32 * HIDDEN * 7168, bytes_accessed=HIDDEN * 7168 * 2, transcendentals=0
        ),
    )(weights[0], factor_init[0])
    new, nxt = pl.pallas_call(
        update_kernel,
        name="update",
        out_shape=(
            jax.ShapeDtypeStruct(weights.shape, BF),
            jax.ShapeDtypeStruct(factor_init.shape, F32),
        ),
        in_specs=[pl.BlockSpec(memory_space=pltpu.VMEM)] * 3,
        out_specs=[pl.BlockSpec(memory_space=pl.ANY)] * 2,
        scratch_shapes=[
            pltpu.VMEM((ZS, HIDDEN, BLOCK), BF),
            pltpu.VMEM((RANK, ZS * BLOCK), F32),
            pltpu.SemaphoreType.DMA((ZS,)),
            pltpu.SemaphoreType.DMA(()),
        ],
        compiler_params=pltpu.CompilerParams(vmem_limit_bytes=32 * 2**20),
        cost_estimate=pl.CostEstimate(
            flops=2 * 128 * HIDDEN * 7168, bytes_accessed=HIDDEN * 7168 * 4, transcendentals=0
        ),
    )(weights, lhs, fac)
    return new, nxt


def solution(mesh):
    in_specs = (P("group", "shard", None), P("group", None, None))
    out_specs = (P("group", "shard", None), P("group", None, None))
    return jax.shard_map(body, mesh=mesh, in_specs=in_specs, out_specs=out_specs, check_vma=False)
```

```python
import jax
import jax.numpy as jnp
from jax import lax
from jax.experimental import pallas as pl
from jax.experimental.pallas import tpu as pltpu
from jax.sharding import PartitionSpec as P

STEPS = 2
RANK = 16
gossip_rate = 0.5

BF = jnp.bfloat16
F32 = jnp.float32
MESH = pl.DeviceIdType.MESH

ZS = 8
BLOCK = 896
SKEW = 384
PART = 512
TILE = 128
HIDDEN = 320
BOTH = 640

ORDER = (4, 3, 5, 2, 6, 1, 7, 0)
NEAR = (0, 1, 7, 2, 6, 3, 5, 4)
GRAM_AT = 7
ALL = tuple((d, e) for d in ORDER for e in (1, 0))
PEERS = tuple((d, e) for d in ORDER for e in (1, 0) if d or e)


def split3(x):
    hi = x.astype(BF)
    rest = x - hi.astype(F32)
    mid = rest.astype(BF)
    lo = (rest - mid.astype(F32)).astype(BF)
    return hi, mid, lo


def pack_gram(square):
    wide = jnp.concatenate([square, jnp.zeros((2 * RANK, TILE - 2 * RANK), F32)], axis=1)
    lane = lax.broadcasted_iota(jnp.int32, (8, TILE), 1)
    packed = jnp.where(lane < RANK, wide[:8], pltpu.roll(wide[8:16], RANK, axis=1))
    packed = jnp.where(lane < 2 * RANK, packed, pltpu.roll(wide[16:24], RANK, axis=1))
    return jnp.where(lane < 3 * RANK, packed, pltpu.roll(wide[24:], 2 * RANK, axis=1))


def inverse_factors(packed):
    rolled = [packed] + [pltpu.roll(packed, TILE - k * RANK, axis=1) for k in range(1, 4)]
    both = jnp.concatenate(rolled, axis=0).reshape(2, RANK, TILE)
    row = lax.broadcasted_iota(jnp.int32, (2, RANK, TILE), 1)
    lane = lax.broadcasted_iota(jnp.int32, (2, RANK, TILE), 2)
    eye = jnp.where(lane - RANK == row, 1.0, 0.0)
    a = jnp.where(lane < RANK, both, eye)
    for k in range(RANK - 1):
        pivot = a[:, k : k + 1, :]
        m = jnp.where(row[:, :, :1] > k, a[:, :, k : k + 1] / pivot[:, :, k : k + 1], 0.0)
        a = a - m * pivot
    diagonal = jnp.sum(jnp.where(lane == row, a, 0.0), axis=2, keepdims=True)
    return a / jnp.sqrt(diagonal)


def apply_lower(inverse, x):
    total = inverse[:, RANK : RANK + 1] * x[0:1, :]
    for k in range(1, RANK):
        total = total + inverse[:, RANK + k : RANK + k + 1] * x[k : k + 1, :]
    return total


def main_kernel(
    w_hbm, f0, lhs_ref, fac_ref,
    w, f, xs, xc, xr, gs, gz, ko, kx, sn, rn, dd, r, bt,
    hop, w_sem, wx_s, wx_r, init_s, init_r, c_s, c_r, x_s, x_r, gz_s, gz_r,
    k_s, k_r, p_s, p_r, r_s, r_r, az_s, az_r, ax_s, ax_r, ag_s, ag_r, ac_s, ac_r,
):
    g = lax.axis_index("group")
    s = lax.axis_index("shard")
    z, xh, c = s // 4, (s // 2) % 2, s % 2
    other = (g, s + 1 - 2 * c)
    left, right = ((g + 7) % 8, s), ((g + 1) % 8, s)

    def peer(d, e):
        return (g, ((z + d) % ZS) * 4 + ((xh + e) % 2) * 2 + c)

    started = []

    def send(src, dst, ss, rs, to):
        copy = pltpu.make_async_remote_copy(
            src_ref=src, dst_ref=dst, send_sem=ss, recv_sem=rs, device_id=to, device_id_type=MESH
        )
        copy.start()
        started.append(copy)
        return copy

    def settle():
        while started:
            started.pop(0).wait_send()

    def columns(b, core):
        return pl.ds(pl.multiple_of(b * BLOCK + core * SKEW, TILE), PART)

    beyond = [((g + k) % 8, s + 1 - 2 * c) for k in (7, 1)]
    barrier = pltpu.get_barrier_semaphore()
    above, below = peer(1, 0), peer(7, 0)
    aside = [((g + k) % 8, peer(0, 1)[1]) for k in (7, 1)]
    greeted = [other, left, right, above, below, peer(0, 1)] + beyond + aside
    for device in greeted:
        pl.semaphore_signal(barrier, inc=1, device_id=device, device_id_type=MESH)

    loads = []
    for b in range(ZS):
        load = pltpu.make_async_copy(w_hbm.at[:, columns(b, c)], w.at[b, c], w_sem.at[b])
        load.start()
        loads.append(load)

    for b in range(ZS):
        for t in range(4):
            tile = pl.ds(pl.multiple_of(b * BLOCK + c * SKEW + t * TILE, TILE), TILE)
            f[0, b, t // 2, t % 2, 1] = f0[:, tile].astype(BF)
    pl.semaphore_wait(barrier, len(greeted))

    first, swaps = [], []
    for b in range(ZS):
        if b % 2 == 0:
            two = pl.ds(b, 2)
            first.append([
                send(
                    f.at[0, two, k, :, 1], f.at[0, two, 1 - k, :, 0],
                    init_s.at[b // 2, k], init_r.at[b // 2, 1 - k], right,
                )
                for k in range(2)
            ])
        swaps.append(send(w_hbm.at[:, columns(b, 1 - c)], w.at[b, c], wx_s.at[b], wx_r.at[b], other))

    def tell(k):
        for way, device in enumerate((above, below)):
            pl.semaphore_signal(hop.at[k, way], inc=1, device_id=device, device_id_type=MESH)

    def hear(k):
        for way in range(2):
            pl.semaphore_wait(hop.at[k, way], 1)

    tell(0)
    for k in range(2):
        hear(k)
        tell(k + 1)
    gathers = {}
    for step in range(STEPS):
        part = jnp.zeros((2 * RANK, BOTH), F32)
        for i, d in enumerate(NEAR):
            if step == 0:
                b = i
                if i == 4:
                    hear(2)
                    tell(3)
                loads[b].wait()
                swaps[b].wait_recv()
                if b % 2 == 0:
                    for copy in first[b // 2]:
                        copy.wait_recv()
            else:
                b = (z + ZS - d) % ZS
                for copy in gathers[d]:
                    copy.wait_recv()
            tiles = []
            for t in range(4):
                k = t // 2
                tile = jnp.concatenate([f[step, b, 1 - k, t % 2, 0], f[step, b, k, t % 2, 1]], axis=0)
                if t == 0:
                    tile = jnp.where(c == 1, jnp.zeros_like(tile), tile)
                tiles.append(tile)
            part = part + lax.dot_general(
                jnp.concatenate(tiles, axis=1), w[b].reshape(BOTH, PART),
                (((1,), (1,)), ((), ())), preferred_element_type=F32,
            )
        xs[step, 0] = part[:RANK]
        xs[step, 1] = part[RANK:]
        swapped = [
            send(xs.at[step, side], xr.at[step, far, 1 - side], x_s.at[step, far, side], x_r.at[step, far, 1 - side], to)
            for side, same in ((1, right), (0, left))
            for far, to in ((0, same), (1, beyond[side]))
        ]
        swapped.append(send(xs.at[step], xc.at[step], c_s.at[step], c_r.at[step], other))
        for copy in swapped:
            copy.wait_recv()
        raw = jnp.concatenate([
            (xr[step, 0, 0] + xr[step, 1, 0]) - (part[:RANK] + xc[step, 0]),
            (part[RANK:] + xc[step, 1]) - (xr[step, 0, 1] + xr[step, 1, 1]),
        ], axis=0)

        stacked = jnp.concatenate(split3(raw), axis=0)
        cross_copies = []
        for i, d in enumerate(ORDER):
            b = (z + d) % ZS
            prod = jnp.dot(stacked, w[b].reshape(BOTH, PART), preferred_element_type=F32)
            prod = prod[: 2 * RANK] + (prod[2 * RANK : 4 * RANK] + prod[4 * RANK :])
            for t in range(2):
                own, over = slice(t * TILE, (t + 1) * TILE), slice((2 + t) * TILE, (3 + t) * TILE)
                ko[step, i, t, 0] = -prod[:RANK, over]
                ko[step, i, t, 1] = prod[RANK:, own]
                sn[step, i, 0, t] = -prod[:RANK, own]
                sn[step, i, 1, t] = prod[RANK:, over]
            cross_copies.append([
                send(ko.at[step, i, 1 - xh], kx.at[step, i], k_s.at[step, i], k_r.at[step, i], peer(0, 1))
            ] + [
                send(
                    sn.at[step, i, side, (xh + far) % 2], rn.at[step, i, far, 1 - side],
                    p_s.at[step, i, far, side], p_r.at[step, i, far, 1 - side], to,
                )
                for far, pair in ((0, (left, right)), (1, aside))
                for side, to in enumerate(pair)
            ])
            if i == GRAM_AT:
                if step == 0:
                    hear(3)
                square = lax.dot_general(
                    raw, raw, (((1,), (1,)), ((), ())),
                    precision=lax.Precision.HIGHEST, preferred_element_type=F32,
                )
                gram = pack_gram(square)
                gs[step, 0] = gram
                gram_copies = [
                    send(gs.at[step, 0], gz.at[step, j], gz_s.at[step, j], gz_r.at[step, j], peer(d2, e2))
                    for j, (d2, e2) in enumerate(PEERS)
                ]

        reduce_copies = []
        for i, d in enumerate(ORDER):
            for copy in cross_copies[i]:
                copy.wait_recv()
            dd[step, i] = ko[step, i, xh] + kx[step, i] + (rn[step, i, 0] + rn[step, i, 1])
            if d:
                reduce_copies.append(send(
                    dd.at[step, i], r.at[step, i], r_s.at[step, i], r_r.at[step, i], peer(d, 0)
                ))

        for j, copy in enumerate(gram_copies):
            copy.wait_recv()
            gram = gram + gz[step, j]
        inverses = inverse_factors(gram)

        total = dd[step, ZS - 1]
        for j, copy in enumerate(reduce_copies):
            copy.wait_recv()
            total = total + r[step, j]

        f[step + 1, z, 0, xh, 0] = apply_lower(inverses[0], total[0]).astype(BF)
        f[step + 1, z, 0, xh, 1] = apply_lower(inverses[1], total[1]).astype(BF)
        piece = f.at[step + 1, z, 0, xh]
        early = len(started)
        along = {
            d: send(piece, piece, az_s.at[step, j], az_r.at[step, j], peer(d, 0))
            for j, d in enumerate(ORDER[:-1])
        }
        for copy in started[:early]:
            copy.wait_send()
        del started[:early]
        if step == STEPS - 1:
            basis = gossip_rate * jnp.concatenate(
                [-apply_lower(inverses[0], raw[:RANK]), apply_lower(inverses[1], raw[RANK:])], axis=0
            )
            terms = [term.astype(F32) for term in split3(basis)]
            bt[...] = jnp.concatenate(terms + [jnp.zeros((2 * RANK, BOTH), F32)], axis=0).T
            lhs_ref[...] = bt[pl.ds(pl.multiple_of(c * HIDDEN, 16), HIDDEN), :].astype(BF)
        gathers = {}
        for i, d in enumerate(NEAR):
            if d:
                along[d].wait_recv()
            b = (z + ZS - d) % ZS
            here = f.at[step + 1, b, 0, xh]
            gathers[d] = [send(here, here, ax_s.at[step, i], ax_r.at[step, i], peer(0, 1))] + [
                send(
                    here.at[side], f.at[step + 1, b, 1, xh, 1 - side],
                    ag_s.at[step, i, far, side], ag_r.at[step, i, far, 1 - side], to,
                )
                for far, pair in ((1, aside), (0, (left, right)))
                for side, to in enumerate(pair)
            ]

    lasts = []
    for i, d in enumerate(NEAR):
        b = (z + ZS - d) % ZS
        for copy in gathers[d]:
            copy.wait_recv()
        lasts.append(send(f.at[STEPS, b], fac_ref.at[c, b], ac_s.at[i], ac_r.at[i], other))
        fac_ref[c, b] = f[STEPS, b]
    settle()
    for copy in lasts:
        copy.wait_recv()


def update_kernel(w_ref, lhs_ref, fac_ref, new_hbm, next_hbm, new, nxt, new_sem, next_sem):
    stores = []
    for b in range(ZS):
        tiles = []
        for core in range(2):
            for t in range(core, 4):
                k = t // 2
                tiles.append(jnp.concatenate(
                    [fac_ref[core, b, 1 - k, t % 2, 0], fac_ref[core, b, k, t % 2, 1]], axis=0
                ))
        fac = jnp.concatenate(tiles, axis=1)
        rhs = jnp.concatenate([fac, fac, fac, jnp.zeros_like(fac)], axis=0)
        delta = jnp.dot(lhs_ref[...], rhs, preferred_element_type=F32)
        columns = slice(b * BLOCK, (b + 1) * BLOCK)
        new[b] = (w_ref[0, :, columns].astype(F32) - delta).astype(BF)
        store = pltpu.make_async_copy(new.at[b], new_hbm.at[0, :, columns], new_sem.at[b])
        store.start()
        stores.append(store)
        nxt[:, columns] = fac[RANK:].astype(F32)
    store = pltpu.make_async_copy(nxt, next_hbm.at[0], next_sem)
    store.start()
    for copy in [*stores, store]:
        copy.wait()


def body(weights, factor_init):
    dma = pltpu.SemaphoreType.DMA
    n = len(PEERS)
    lhs, fac = pl.pallas_call(
        main_kernel,
        name="rounds",
        out_shape=(
            jax.ShapeDtypeStruct((HIDDEN, TILE), BF),
            jax.ShapeDtypeStruct((2, ZS, 2, 2, 2, RANK, TILE), BF),
        ),
        in_specs=[pl.BlockSpec(memory_space=pltpu.HBM), pl.BlockSpec(memory_space=pltpu.VMEM)],
        out_specs=[pl.BlockSpec(memory_space=pltpu.VMEM)] * 2,
        scratch_shapes=[
            pltpu.VMEM((ZS, 2, HIDDEN, PART), BF),
            pltpu.VMEM((STEPS + 1, ZS, 2, 2, 2, RANK, TILE), BF),
            pltpu.VMEM((STEPS, 2, RANK, BOTH), F32),
            pltpu.VMEM((STEPS, 2, RANK, BOTH), F32),
            pltpu.VMEM((STEPS, 2, 2, RANK, BOTH), F32),
            pltpu.VMEM((STEPS, 2, 8, TILE), F32),
            pltpu.VMEM((STEPS, n, 8, TILE), F32),
            pltpu.VMEM((STEPS, ZS, 2, 2, RANK, TILE), F32),
            pltpu.VMEM((STEPS, ZS, 2, RANK, TILE), F32),
            pltpu.VMEM((STEPS, ZS, 2, 2, RANK, TILE), F32),
            pltpu.VMEM((STEPS, ZS, 2, 2, RANK, TILE), F32),
            pltpu.VMEM((STEPS, ZS, 2, RANK, TILE), F32),
            pltpu.VMEM((STEPS, ZS - 1, 2, RANK, TILE), F32),
            pltpu.VMEM((BOTH, TILE), F32),
            pltpu.SemaphoreType.REGULAR((4, 2)),
            dma((ZS,)),
            dma((ZS,)), dma((ZS,)),
            dma((ZS // 2, 2)), dma((ZS // 2, 2)),
            dma((STEPS,)), dma((STEPS,)),
            dma((STEPS, 2, 2)), dma((STEPS, 2, 2)),
            dma((STEPS, n)), dma((STEPS, n)),
            dma((STEPS, ZS)), dma((STEPS, ZS)),
            dma((STEPS, ZS, 2, 2)), dma((STEPS, ZS, 2, 2)),
            dma((STEPS, ZS - 1)), dma((STEPS, ZS - 1)),
            dma((STEPS, ZS - 1)), dma((STEPS, ZS - 1)),
            dma((STEPS, ZS)), dma((STEPS, ZS)),
            dma((STEPS, ZS, 2, 2)), dma((STEPS, ZS, 2, 2)),
            dma((ZS,)), dma((ZS,)),
        ],
        compiler_params=pltpu.CompilerParams(
            collective_id=0, has_side_effects=True, vmem_limit_bytes=52 * 2**20
        ),
        cost_estimate=pl.CostEstimate(
            flops=10 * 32 * HIDDEN * 7168, bytes_accessed=HIDDEN * 7168 * 2, transcendentals=0
        ),
    )(weights[0], factor_init[0])
    new, nxt = pl.pallas_call(
        update_kernel,
        name="update",
        out_shape=(
            jax.ShapeDtypeStruct(weights.shape, BF),
            jax.ShapeDtypeStruct(factor_init.shape, F32),
        ),
        in_specs=[pl.BlockSpec(memory_space=pltpu.VMEM)] * 3,
        out_specs=[pl.BlockSpec(memory_space=pl.ANY)] * 2,
        scratch_shapes=[
            pltpu.VMEM((ZS, HIDDEN, BLOCK), BF),
            pltpu.VMEM((RANK, ZS * BLOCK), F32),
            pltpu.SemaphoreType.DMA((ZS,)),
            pltpu.SemaphoreType.DMA(()),
        ],
        compiler_params=pltpu.CompilerParams(vmem_limit_bytes=32 * 2**20),
        cost_estimate=pl.CostEstimate(
            flops=2 * 128 * HIDDEN * 7168, bytes_accessed=HIDDEN * 7168 * 4, transcendentals=0
        ),
    )(weights, lhs, fac)
    return new, nxt


def solution(mesh):
    in_specs = (P("group", "shard", None), P("group", None, None))
    out_specs = (P("group", "shard", None), P("group", None, None))
    return jax.shard_map(body, mesh=mesh, in_specs=in_specs, out_specs=out_specs, check_vma=False)
```

```python
import jax
import jax.numpy as jnp
from jax import lax
from jax.experimental import pallas as pl
from jax.experimental.pallas import tpu as pltpu
from jax.sharding import PartitionSpec as P

STEPS = 2
RANK = 16
gossip_rate = 0.5

BF = jnp.bfloat16
F32 = jnp.float32
MESH = pl.DeviceIdType.MESH

ZS = 8
BLOCK = 896
SKEW = 384
PART = 512
TILE = 128
HIDDEN = 320
BOTH = 640

ORDER = (4, 3, 5, 2, 6, 1, 7, 0)
NEAR = (0, 1, 7, 2, 6, 3, 5, 4)
GRAM_AT = 7
ALL = tuple((d, e) for d in ORDER for e in (1, 0))
PEERS = tuple((d, e) for d in ORDER for e in (1, 0) if d or e)


def split3(x):
    hi = x.astype(BF)
    rest = x - hi.astype(F32)
    mid = rest.astype(BF)
    lo = (rest - mid.astype(F32)).astype(BF)
    return hi, mid, lo


def pack_gram(square):
    wide = jnp.concatenate([square, jnp.zeros((2 * RANK, TILE - 2 * RANK), F32)], axis=1)
    lane = lax.broadcasted_iota(jnp.int32, (8, TILE), 1)
    packed = jnp.where(lane < RANK, wide[:8], pltpu.roll(wide[8:16], RANK, axis=1))
    packed = jnp.where(lane < 2 * RANK, packed, pltpu.roll(wide[16:24], RANK, axis=1))
    return jnp.where(lane < 3 * RANK, packed, pltpu.roll(wide[24:], 2 * RANK, axis=1))


def inverse_factors(packed):
    rolled = [packed] + [pltpu.roll(packed, TILE - k * RANK, axis=1) for k in range(1, 4)]
    both = jnp.concatenate(rolled, axis=0).reshape(2, RANK, TILE)
    row = lax.broadcasted_iota(jnp.int32, (2, RANK, TILE), 1)
    lane = lax.broadcasted_iota(jnp.int32, (2, RANK, TILE), 2)
    eye = jnp.where(lane - RANK == row, 1.0, 0.0)
    a = jnp.where(lane < RANK, both, eye)
    for k in range(RANK - 1):
        pivot = a[:, k : k + 1, :]
        m = jnp.where(row[:, :, :1] > k, a[:, :, k : k + 1] / pivot[:, :, k : k + 1], 0.0)
        a = a - m * pivot
    diagonal = jnp.sum(jnp.where(lane == row, a, 0.0), axis=2, keepdims=True)
    return a / jnp.sqrt(diagonal)


def apply_lower(inverse, x):
    total = inverse[:, RANK : RANK + 1] * x[0:1, :]
    for k in range(1, RANK):
        total = total + inverse[:, RANK + k : RANK + k + 1] * x[k : k + 1, :]
    return total


def main_kernel(
    w_hbm, f0_hbm, lhs_ref, fac_ref,
    w, f0, f, xs, xc, xr, gs, gz, ko, kx, sn, rn, dd, r, bt,
    hop, w_sem, f0_sem, wx_s, wx_r, init_s, init_r, c_s, c_r, x_s, x_r, gz_s, gz_r,
    k_s, k_r, p_s, p_r, r_s, r_r, az_s, az_r, ax_s, ax_r, ag_s, ag_r, ac_s, ac_r,
):
    g = lax.axis_index("group")
    s = lax.axis_index("shard")
    z, xh, c = s // 4, (s // 2) % 2, s % 2
    other = (g, s + 1 - 2 * c)
    left, right = ((g + 7) % 8, s), ((g + 1) % 8, s)

    def peer(d, e):
        return (g, ((z + d) % ZS) * 4 + ((xh + e) % 2) * 2 + c)

    started = []

    def send(src, dst, ss, rs, to):
        copy = pltpu.make_async_remote_copy(
            src_ref=src, dst_ref=dst, send_sem=ss, recv_sem=rs, device_id=to, device_id_type=MESH
        )
        copy.start()
        started.append(copy)
        return copy

    def settle():
        while started:
            started.pop(0).wait_send()

    def columns(b, core):
        return pl.ds(pl.multiple_of(b * BLOCK + core * SKEW, TILE), PART)

    beyond = [((g + k) % 8, s + 1 - 2 * c) for k in (7, 1)]
    f0_load = pltpu.make_async_copy(f0_hbm, f0, f0_sem)
    f0_load.start()
    barrier = pltpu.get_barrier_semaphore()
    above, below = peer(1, 0), peer(7, 0)
    aside = [((g + k) % 8, peer(0, 1)[1]) for k in (7, 1)]
    greeted = [other, left, right, above, below, peer(0, 1)] + beyond + aside
    for device in greeted:
        pl.semaphore_signal(barrier, inc=1, device_id=device, device_id_type=MESH)

    loads = []
    for b in range(ZS):
        load = pltpu.make_async_copy(w_hbm.at[:, columns(b, c)], w.at[b, c], w_sem.at[b])
        load.start()
        loads.append(load)

    def tell(k):
        for way, device in enumerate((above, below)):
            pl.semaphore_signal(hop.at[k, way], inc=1, device_id=device, device_id_type=MESH)

    def hear(k):
        for way in range(2):
            pl.semaphore_wait(hop.at[k, way], 1)

    pl.semaphore_wait(barrier, len(greeted))
    tell(0)

    swaps = [
        send(w_hbm.at[:, columns(b, 1 - c)], w.at[b, c], wx_s.at[b], wx_r.at[b], other)
        for b in range(ZS)
    ]

    f0_load.wait()
    first = []
    for b in range(ZS):
        for t in range(4):
            tile = pl.ds(pl.multiple_of(b * BLOCK + c * SKEW + t * TILE, TILE), TILE)
            f[0, b, t // 2, t % 2, 1] = f0[:, tile].astype(BF)
        if b % 2:
            two = pl.ds(b - 1, 2)
            first.append([
                send(
                    f.at[0, two, k, :, 1], f.at[0, two, 1 - k, :, 0],
                    init_s.at[b // 2, k], init_r.at[b // 2, 1 - k], right,
                )
                for k in range(2)
            ])

    for k in range(2):
        hear(k)
        tell(k + 1)
    gathers = {}
    for step in range(STEPS):
        part = jnp.zeros((2 * RANK, BOTH), F32)
        for i, d in enumerate(NEAR):
            if step == 0:
                b = i
                if i == 4:
                    hear(2)
                    tell(3)
                loads[b].wait()
                swaps[b].wait_recv()
                if b % 2 == 0:
                    for copy in first[b // 2]:
                        copy.wait_recv()
            else:
                b = (z + ZS - d) % ZS
                for copy in gathers[d]:
                    copy.wait_recv()
            tiles = []
            for t in range(4):
                k = t // 2
                tile = jnp.concatenate([f[step, b, 1 - k, t % 2, 0], f[step, b, k, t % 2, 1]], axis=0)
                if t == 0:
                    tile = jnp.where(c == 1, jnp.zeros_like(tile), tile)
                tiles.append(tile)
            part = part + lax.dot_general(
                jnp.concatenate(tiles, axis=1), w[b].reshape(BOTH, PART),
                (((1,), (1,)), ((), ())), preferred_element_type=F32,
            )
        xs[step, 0] = part[:RANK]
        xs[step, 1] = part[RANK:]
        swapped = [
            send(xs.at[step, side], xr.at[step, far, 1 - side], x_s.at[step, far, side], x_r.at[step, far, 1 - side], to)
            for side, same in ((1, right), (0, left))
            for far, to in ((0, same), (1, beyond[side]))
        ]
        swapped.append(send(xs.at[step], xc.at[step], c_s.at[step], c_r.at[step], other))
        for copy in swapped:
            copy.wait_recv()
        raw = jnp.concatenate([
            (xr[step, 0, 0] + xr[step, 1, 0]) - (part[:RANK] + xc[step, 0]),
            (part[RANK:] + xc[step, 1]) - (xr[step, 0, 1] + xr[step, 1, 1]),
        ], axis=0)

        stacked = jnp.concatenate(split3(raw), axis=0)
        cross_copies = []
        for i, d in enumerate(ORDER):
            b = (z + d) % ZS
            prod = jnp.dot(stacked, w[b].reshape(BOTH, PART), preferred_element_type=F32)
            prod = prod[: 2 * RANK] + (prod[2 * RANK : 4 * RANK] + prod[4 * RANK :])
            for t in range(2):
                own, over = slice(t * TILE, (t + 1) * TILE), slice((2 + t) * TILE, (3 + t) * TILE)
                ko[step, i, t, 0] = -prod[:RANK, over]
                ko[step, i, t, 1] = prod[RANK:, own]
                sn[step, i, 0, t] = -prod[:RANK, own]
                sn[step, i, 1, t] = prod[RANK:, over]
            cross_copies.append([
                send(ko.at[step, i, 1 - xh], kx.at[step, i], k_s.at[step, i], k_r.at[step, i], peer(0, 1))
            ] + [
                send(
                    sn.at[step, i, side, (xh + far) % 2], rn.at[step, i, far, 1 - side],
                    p_s.at[step, i, far, side], p_r.at[step, i, far, 1 - side], to,
                )
                for far, pair in ((0, (left, right)), (1, aside))
                for side, to in enumerate(pair)
            ])
            if i == GRAM_AT:
                if step == 0:
                    hear(3)
                square = lax.dot_general(
                    raw, raw, (((1,), (1,)), ((), ())),
                    precision=lax.Precision.HIGHEST, preferred_element_type=F32,
                )
                gram = pack_gram(square)
                gs[step, 0] = gram
                gram_copies = [
                    send(gs.at[step, 0], gz.at[step, j], gz_s.at[step, j], gz_r.at[step, j], peer(d2, e2))
                    for j, (d2, e2) in enumerate(PEERS)
                ]

        reduce_copies = []
        for i, d in enumerate(ORDER):
            for copy in cross_copies[i]:
                copy.wait_recv()
            dd[step, i] = ko[step, i, xh] + kx[step, i] + (rn[step, i, 0] + rn[step, i, 1])
            if d:
                reduce_copies.append(send(
                    dd.at[step, i], r.at[step, i], r_s.at[step, i], r_r.at[step, i], peer(d, 0)
                ))

        for j, copy in enumerate(gram_copies):
            copy.wait_recv()
            gram = gram + gz[step, j]
        inverses = inverse_factors(gram)

        total = dd[step, ZS - 1]
        for j, copy in enumerate(reduce_copies):
            copy.wait_recv()
            total = total + r[step, j]

        f[step + 1, z, 0, xh, 0] = apply_lower(inverses[0], total[0]).astype(BF)
        f[step + 1, z, 0, xh, 1] = apply_lower(inverses[1], total[1]).astype(BF)
        piece = f.at[step + 1, z, 0, xh]
        early = len(started)
        along = {
            d: send(piece, piece, az_s.at[step, j], az_r.at[step, j], peer(d, 0))
            for j, d in enumerate(ORDER[:-1])
        }
        for copy in started[:early]:
            copy.wait_send()
        del started[:early]
        if step == STEPS - 1:
            basis = gossip_rate * jnp.concatenate(
                [-apply_lower(inverses[0], raw[:RANK]), apply_lower(inverses[1], raw[RANK:])], axis=0
            )
            terms = [term.astype(F32) for term in split3(basis)]
            bt[...] = jnp.concatenate(terms + [jnp.zeros((2 * RANK, BOTH), F32)], axis=0).T
            lhs_ref[...] = bt[pl.ds(pl.multiple_of(c * HIDDEN, 16), HIDDEN), :].astype(BF)
        gathers = {}
        for i, d in enumerate(NEAR):
            if d:
                along[d].wait_recv()
            b = (z + ZS - d) % ZS
            here = f.at[step + 1, b, 0, xh]
            gathers[d] = [send(here, here, ax_s.at[step, i], ax_r.at[step, i], peer(0, 1))] + [
                send(
                    here.at[side], f.at[step + 1, b, 1, xh, 1 - side],
                    ag_s.at[step, i, far, side], ag_r.at[step, i, far, 1 - side], to,
                )
                for far, pair in ((1, aside), (0, (left, right)))
                for side, to in enumerate(pair)
            ]

    lasts = []
    for i, d in enumerate(NEAR):
        b = (z + ZS - d) % ZS
        for copy in gathers[d]:
            copy.wait_recv()
        lasts.append(send(f.at[STEPS, b], fac_ref.at[c, b], ac_s.at[i], ac_r.at[i], other))
        fac_ref[c, b] = f[STEPS, b]
    settle()
    for copy in lasts:
        copy.wait_recv()


def update_kernel(w_ref, lhs_ref, fac_ref, new_hbm, next_hbm, new, nxt, new_sem, next_sem):
    stores = []
    for b in range(ZS):
        tiles = []
        for core in range(2):
            for t in range(core, 4):
                k = t // 2
                tiles.append(jnp.concatenate(
                    [fac_ref[core, b, 1 - k, t % 2, 0], fac_ref[core, b, k, t % 2, 1]], axis=0
                ))
        fac = jnp.concatenate(tiles, axis=1)
        rhs = jnp.concatenate([fac, fac, fac, jnp.zeros_like(fac)], axis=0)
        delta = jnp.dot(lhs_ref[...], rhs, preferred_element_type=F32)
        columns = slice(b * BLOCK, (b + 1) * BLOCK)
        new[b] = (w_ref[0, :, columns].astype(F32) - delta).astype(BF)
        store = pltpu.make_async_copy(new.at[b], new_hbm.at[0, :, columns], new_sem.at[b])
        store.start()
        stores.append(store)
        nxt[:, columns] = fac[RANK:].astype(F32)
    store = pltpu.make_async_copy(nxt, next_hbm.at[0], next_sem)
    store.start()
    for copy in [*stores, store]:
        copy.wait()


def body(weights, factor_init):
    dma = pltpu.SemaphoreType.DMA
    n = len(PEERS)
    lhs, fac = pl.pallas_call(
        main_kernel,
        name="rounds",
        out_shape=(
            jax.ShapeDtypeStruct((HIDDEN, TILE), BF),
            jax.ShapeDtypeStruct((2, ZS, 2, 2, 2, RANK, TILE), BF),
        ),
        in_specs=[pl.BlockSpec(memory_space=pltpu.HBM)] * 2,
        out_specs=[pl.BlockSpec(memory_space=pltpu.VMEM)] * 2,
        scratch_shapes=[
            pltpu.VMEM((ZS, 2, HIDDEN, PART), BF),
            pltpu.VMEM((RANK, ZS * BLOCK), F32),
            pltpu.VMEM((STEPS + 1, ZS, 2, 2, 2, RANK, TILE), BF),
            pltpu.VMEM((STEPS, 2, RANK, BOTH), F32),
            pltpu.VMEM((STEPS, 2, RANK, BOTH), F32),
            pltpu.VMEM((STEPS, 2, 2, RANK, BOTH), F32),
            pltpu.VMEM((STEPS, 2, 8, TILE), F32),
            pltpu.VMEM((STEPS, n, 8, TILE), F32),
            pltpu.VMEM((STEPS, ZS, 2, 2, RANK, TILE), F32),
            pltpu.VMEM((STEPS, ZS, 2, RANK, TILE), F32),
            pltpu.VMEM((STEPS, ZS, 2, 2, RANK, TILE), F32),
            pltpu.VMEM((STEPS, ZS, 2, 2, RANK, TILE), F32),
            pltpu.VMEM((STEPS, ZS, 2, RANK, TILE), F32),
            pltpu.VMEM((STEPS, ZS - 1, 2, RANK, TILE), F32),
            pltpu.VMEM((BOTH, TILE), F32),
            pltpu.SemaphoreType.REGULAR((4, 2)),
            dma((ZS,)), dma(()),
            dma((ZS,)), dma((ZS,)),
            dma((ZS // 2, 2)), dma((ZS // 2, 2)),
            dma((STEPS,)), dma((STEPS,)),
            dma((STEPS, 2, 2)), dma((STEPS, 2, 2)),
            dma((STEPS, n)), dma((STEPS, n)),
            dma((STEPS, ZS)), dma((STEPS, ZS)),
            dma((STEPS, ZS, 2, 2)), dma((STEPS, ZS, 2, 2)),
            dma((STEPS, ZS - 1)), dma((STEPS, ZS - 1)),
            dma((STEPS, ZS - 1)), dma((STEPS, ZS - 1)),
            dma((STEPS, ZS)), dma((STEPS, ZS)),
            dma((STEPS, ZS, 2, 2)), dma((STEPS, ZS, 2, 2)),
            dma((ZS,)), dma((ZS,)),
        ],
        compiler_params=pltpu.CompilerParams(
            collective_id=0, has_side_effects=True, vmem_limit_bytes=52 * 2**20
        ),
        cost_estimate=pl.CostEstimate(
            flops=10 * 32 * HIDDEN * 7168, bytes_accessed=HIDDEN * 7168 * 2, transcendentals=0
        ),
    )(*(pltpu.with_memory_space_constraint(x, pltpu.HBM) for x in (weights[0], factor_init[0])))
    new, nxt = pl.pallas_call(
        update_kernel,
        name="update",
        out_shape=(
            jax.ShapeDtypeStruct(weights.shape, BF),
            jax.ShapeDtypeStruct(factor_init.shape, F32),
        ),
        in_specs=[pl.BlockSpec(memory_space=pltpu.VMEM)] * 3,
        out_specs=[pl.BlockSpec(memory_space=pl.ANY)] * 2,
        scratch_shapes=[
            pltpu.VMEM((ZS, HIDDEN, BLOCK), BF),
            pltpu.VMEM((RANK, ZS * BLOCK), F32),
            pltpu.SemaphoreType.DMA((ZS,)),
            pltpu.SemaphoreType.DMA(()),
        ],
        compiler_params=pltpu.CompilerParams(vmem_limit_bytes=32 * 2**20),
        cost_estimate=pl.CostEstimate(
            flops=2 * 128 * HIDDEN * 7168, bytes_accessed=HIDDEN * 7168 * 4, transcendentals=0
        ),
    )(weights, lhs, fac)
    return new, nxt


def solution(mesh):
    in_specs = (P("group", "shard", None), P("group", None, None))
    out_specs = (P("group", "shard", None), P("group", None, None))
    return jax.shard_map(body, mesh=mesh, in_specs=in_specs, out_specs=out_specs, check_vma=False)
```

```python
import jax
import jax.numpy as jnp
from jax import lax
from jax.experimental import pallas as pl
from jax.experimental.pallas import tpu as pltpu
from jax.sharding import PartitionSpec as P

STEPS = 2
RANK = 16
gossip_rate = 0.5

BF = jnp.bfloat16
F32 = jnp.float32
MESH = pl.DeviceIdType.MESH

ZS = 8
BLOCK = 896
SKEW = 384
PART = 512
TILE = 128
HIDDEN = 320
BOTH = 640

ORDER = (4, 3, 5, 2, 6, 1, 7, 0)
NEAR = (0, 1, 7, 2, 6, 3, 5, 4)
GRAM_ON = 1
GRAM_AT = 2
ALL = tuple((d, e) for d in ORDER for e in (1, 0))
PEERS = tuple((d, e) for d in ORDER for e in (1, 0) if d or e)


def split3(x):
    hi = x.astype(BF)
    rest = x - hi.astype(F32)
    mid = rest.astype(BF)
    lo = (rest - mid.astype(F32)).astype(BF)
    return hi, mid, lo


def pack_gram(square):
    wide = jnp.concatenate([square, jnp.zeros((2 * RANK, TILE - 2 * RANK), F32)], axis=1)
    lane = lax.broadcasted_iota(jnp.int32, (8, TILE), 1)
    packed = jnp.where(lane < RANK, wide[:8], pltpu.roll(wide[8:16], RANK, axis=1))
    packed = jnp.where(lane < 2 * RANK, packed, pltpu.roll(wide[16:24], RANK, axis=1))
    return jnp.where(lane < 3 * RANK, packed, pltpu.roll(wide[24:], 2 * RANK, axis=1))


def inverse_factors(packed):
    rolled = [packed] + [pltpu.roll(packed, TILE - k * RANK, axis=1) for k in range(1, 4)]
    both = jnp.concatenate(rolled, axis=0).reshape(2, RANK, TILE)
    row = lax.broadcasted_iota(jnp.int32, (2, RANK, TILE), 1)
    lane = lax.broadcasted_iota(jnp.int32, (2, RANK, TILE), 2)
    eye = jnp.where(lane - RANK == row, 1.0, 0.0)
    a = jnp.where(lane < RANK, both, eye)
    for k in range(RANK - 1):
        pivot = a[:, k : k + 1, :]
        m = jnp.where(row[:, :, :1] > k, a[:, :, k : k + 1] / pivot[:, :, k : k + 1], 0.0)
        a = a - m * pivot
    diagonal = jnp.sum(jnp.where(lane == row, a, 0.0), axis=2, keepdims=True)
    return a / jnp.sqrt(diagonal)


def apply_lower(inverse, x):
    total = inverse[:, RANK : RANK + 1] * x[0:1, :]
    for k in range(1, RANK):
        total = total + inverse[:, RANK + k : RANK + k + 1] * x[k : k + 1, :]
    return total


def main_kernel(
    w_hbm, f0_hbm, lhs_ref, fac_ref,
    w, f0, f, xs, xc, xr, gs, gx, gz, ko, kx, sn, rn, dd, r, bt,
    hop, w_sem, f0_sem, wx_s, wx_r, init_s, init_r, c_s, c_r, x_s, x_r, gx_s, gx_r, gz_s, gz_r,
    k_s, k_r, p_s, p_r, r_s, r_r, az_s, az_r, ax_s, ax_r, ag_s, ag_r, ac_s, ac_r,
):
    g = lax.axis_index("group")
    s = lax.axis_index("shard")
    z, xh, c = s // 4, (s // 2) % 2, s % 2
    other = (g, s + 1 - 2 * c)
    left, right = ((g + 7) % 8, s), ((g + 1) % 8, s)

    def peer(d, e):
        return (g, ((z + d) % ZS) * 4 + ((xh + e) % 2) * 2 + c)

    started = []

    def send(src, dst, ss, rs, to):
        copy = pltpu.make_async_remote_copy(
            src_ref=src, dst_ref=dst, send_sem=ss, recv_sem=rs, device_id=to, device_id_type=MESH
        )
        copy.start()
        started.append(copy)
        return copy

    def settle():
        while started:
            started.pop(0).wait_send()

    def columns(b, core):
        return pl.ds(pl.multiple_of(b * BLOCK + core * SKEW, TILE), PART)

    beyond = [((g + k) % 8, s + 1 - 2 * c) for k in (7, 1)]
    f0_load = pltpu.make_async_copy(f0_hbm, f0, f0_sem)
    f0_load.start()
    barrier = pltpu.get_barrier_semaphore()
    above, below = peer(1, 0), peer(7, 0)
    aside = [((g + k) % 8, peer(0, 1)[1]) for k in (7, 1)]
    greeted = [other, left, right, above, below, peer(0, 1)] + beyond + aside
    for device in greeted:
        pl.semaphore_signal(barrier, inc=1, device_id=device, device_id_type=MESH)

    loads = []
    for b in range(ZS):
        load = pltpu.make_async_copy(w_hbm.at[:, columns(b, c)], w.at[b, c], w_sem.at[b])
        load.start()
        loads.append(load)

    def tell(k):
        for way, device in enumerate((above, below)):
            pl.semaphore_signal(hop.at[k, way], inc=1, device_id=device, device_id_type=MESH)

    def hear(k):
        for way in range(2):
            pl.semaphore_wait(hop.at[k, way], 1)

    pl.semaphore_wait(barrier, len(greeted))
    tell(0)

    swaps = [
        send(w_hbm.at[:, columns(b, 1 - c)], w.at[b, c], wx_s.at[b], wx_r.at[b], other)
        for b in range(ZS)
    ]

    f0_load.wait()
    first = []
    for b in range(ZS):
        for t in range(4):
            tile = pl.ds(pl.multiple_of(b * BLOCK + c * SKEW + t * TILE, TILE), TILE)
            f[0, b, t // 2, t % 2, 1] = f0[:, tile].astype(BF)
        if b % 2:
            two = pl.ds(b - 1, 2)
            first.append([
                send(
                    f.at[0, two, k, :, 1], f.at[0, two, 1 - k, :, 0],
                    init_s.at[b // 2, k], init_r.at[b // 2, 1 - k], right,
                )
                for k in range(2)
            ])

    for k in range(2):
        hear(k)
        tell(k + 1)
    gathers = {}
    for step in range(STEPS):
        part = jnp.zeros((2 * RANK, BOTH), F32)
        for i, d in enumerate(NEAR):
            if step == 0:
                b = i
                if i == 4:
                    hear(2)
                    tell(3)
                loads[b].wait()
                swaps[b].wait_recv()
                if b % 2 == 0:
                    for copy in first[b // 2]:
                        copy.wait_recv()
            else:
                b = (z + ZS - d) % ZS
                for copy in gathers[d]:
                    copy.wait_recv()
            tiles = []
            for t in range(4):
                k = t // 2
                tile = jnp.concatenate([f[step, b, 1 - k, t % 2, 0], f[step, b, k, t % 2, 1]], axis=0)
                if t == 0:
                    tile = jnp.where(c == 1, jnp.zeros_like(tile), tile)
                tiles.append(tile)
            part = part + lax.dot_general(
                jnp.concatenate(tiles, axis=1), w[b].reshape(BOTH, PART),
                (((1,), (1,)), ((), ())), preferred_element_type=F32,
            )
        xs[step, 0] = part[:RANK]
        xs[step, 1] = part[RANK:]
        swapped = [
            send(xs.at[step, side], xr.at[step, far, 1 - side], x_s.at[step, far, side], x_r.at[step, far, 1 - side], to)
            for side, same in ((1, right), (0, left))
            for far, to in ((0, same), (1, beyond[side]))
        ]
        swapped.append(send(xs.at[step], xc.at[step], c_s.at[step], c_r.at[step], other))
        for copy in swapped:
            copy.wait_recv()
        raw = jnp.concatenate([
            (xr[step, 0, 0] + xr[step, 1, 0]) - (part[:RANK] + xc[step, 0]),
            (part[RANK:] + xc[step, 1]) - (xr[step, 0, 1] + xr[step, 1, 1]),
        ], axis=0)

        stacked = jnp.concatenate(split3(raw), axis=0)
        cross_copies = []
        for i, d in enumerate(ORDER):
            b = (z + d) % ZS
            prod = jnp.dot(stacked, w[b].reshape(BOTH, PART), preferred_element_type=F32)
            prod = prod[: 2 * RANK] + (prod[2 * RANK : 4 * RANK] + prod[4 * RANK :])
            for t in range(2):
                own, over = slice(t * TILE, (t + 1) * TILE), slice((2 + t) * TILE, (3 + t) * TILE)
                ko[step, i, t, 0] = -prod[:RANK, over]
                ko[step, i, t, 1] = prod[RANK:, own]
                sn[step, i, 0, t] = -prod[:RANK, own]
                sn[step, i, 1, t] = prod[RANK:, over]
            cross_copies.append([
                send(ko.at[step, i, 1 - xh], kx.at[step, i], k_s.at[step, i], k_r.at[step, i], peer(0, 1))
            ] + [
                send(
                    sn.at[step, i, side, (xh + far) % 2], rn.at[step, i, far, 1 - side],
                    p_s.at[step, i, far, side], p_r.at[step, i, far, 1 - side], to,
                )
                for far, pair in ((0, (left, right)), (1, aside))
                for side, to in enumerate(pair)
            ])
            if i == GRAM_AT:
                if step == 0:
                    hear(3)
                square = lax.dot_general(
                    raw, raw, (((1,), (1,)), ((), ())),
                    precision=lax.Precision.HIGHEST, preferred_element_type=F32,
                )
                gram = pack_gram(square)
                gs[step, 0] = gram
                gram_x = send(gs.at[step, 0], gx.at[step], gx_s.at[step], gx_r.at[step], peer(0, 1))

        reduce_copies = []
        for i, d in enumerate(ORDER):
            if i == GRAM_ON:
                gram_x.wait_recv()
                gram = gram + gx[step]
                gs[step, 1] = gram
                gram_copies = [
                    send(gs.at[step, 1], gz.at[step, j], gz_s.at[step, j], gz_r.at[step, j], peer(d2, 0))
                    for j, d2 in enumerate(ORDER[:-1])
                ]
            for copy in cross_copies[i]:
                copy.wait_recv()
            dd[step, i] = ko[step, i, xh] + kx[step, i] + (rn[step, i, 0] + rn[step, i, 1])
            if d:
                reduce_copies.append(send(
                    dd.at[step, i], r.at[step, i], r_s.at[step, i], r_r.at[step, i], peer(d, 0)
                ))

        for j, copy in enumerate(gram_copies):
            copy.wait_recv()
            gram = gram + gz[step, j]
        inverses = inverse_factors(gram)

        total = dd[step, ZS - 1]
        for j, copy in enumerate(reduce_copies):
            copy.wait_recv()
            total = total + r[step, j]

        f[step + 1, z, 0, xh, 0] = apply_lower(inverses[0], total[0]).astype(BF)
        f[step + 1, z, 0, xh, 1] = apply_lower(inverses[1], total[1]).astype(BF)
        piece = f.at[step + 1, z, 0, xh]
        early = len(started)
        along = {
            d: send(piece, piece, az_s.at[step, j], az_r.at[step, j], peer(d, 0))
            for j, d in enumerate(ORDER[:-1])
        }
        for copy in started[:early]:
            copy.wait_send()
        del started[:early]
        if step == STEPS - 1:
            basis = gossip_rate * jnp.concatenate(
                [-apply_lower(inverses[0], raw[:RANK]), apply_lower(inverses[1], raw[RANK:])], axis=0
            )
            terms = [term.astype(F32) for term in split3(basis)]
            bt[...] = jnp.concatenate(terms + [jnp.zeros((2 * RANK, BOTH), F32)], axis=0).T
            lhs_ref[...] = bt[pl.ds(pl.multiple_of(c * HIDDEN, 16), HIDDEN), :].astype(BF)
        gathers = {}
        for i, d in enumerate(NEAR):
            if d:
                along[d].wait_recv()
            b = (z + ZS - d) % ZS
            here = f.at[step + 1, b, 0, xh]
            gathers[d] = [
                send(
                    here.at[side], f.at[step + 1, b, 1, xh, 1 - side],
                    ag_s.at[step, i, far, side], ag_r.at[step, i, far, 1 - side], to,
                )
                for far, pair in ((0, (left, right)), (1, aside))
                for side, to in enumerate(pair)
            ] + [send(here, here, ax_s.at[step, i], ax_r.at[step, i], peer(0, 1))]

    lasts = []
    for i, d in enumerate(NEAR):
        b = (z + ZS - d) % ZS
        for copy in gathers[d]:
            copy.wait_recv()
        lasts.append(send(f.at[STEPS, b], fac_ref.at[c, b], ac_s.at[i], ac_r.at[i], other))
        fac_ref[c, b] = f[STEPS, b]
    settle()
    for copy in lasts:
        copy.wait_recv()


def update_kernel(w_ref, lhs_ref, fac_ref, new_hbm, next_hbm, new, nxt, new_sem, next_sem):
    stores = []
    for b in range(ZS):
        tiles = []
        for core in range(2):
            for t in range(core, 4):
                k = t // 2
                tiles.append(jnp.concatenate(
                    [fac_ref[core, b, 1 - k, t % 2, 0], fac_ref[core, b, k, t % 2, 1]], axis=0
                ))
        fac = jnp.concatenate(tiles, axis=1)
        rhs = jnp.concatenate([fac, fac, fac, jnp.zeros_like(fac)], axis=0)
        delta = jnp.dot(lhs_ref[...], rhs, preferred_element_type=F32)
        columns = slice(b * BLOCK, (b + 1) * BLOCK)
        new[b] = (w_ref[0, :, columns].astype(F32) - delta).astype(BF)
        store = pltpu.make_async_copy(new.at[b], new_hbm.at[0, :, columns], new_sem.at[b])
        store.start()
        stores.append(store)
        nxt[:, columns] = fac[RANK:].astype(F32)
    store = pltpu.make_async_copy(nxt, next_hbm.at[0], next_sem)
    store.start()
    for copy in [*stores, store]:
        copy.wait()


def body(weights, factor_init):
    dma = pltpu.SemaphoreType.DMA
    n = len(PEERS)
    lhs, fac = pl.pallas_call(
        main_kernel,
        name="rounds",
        out_shape=(
            jax.ShapeDtypeStruct((HIDDEN, TILE), BF),
            jax.ShapeDtypeStruct((2, ZS, 2, 2, 2, RANK, TILE), BF),
        ),
        in_specs=[pl.BlockSpec(memory_space=pltpu.HBM)] * 2,
        out_specs=[pl.BlockSpec(memory_space=pltpu.VMEM)] * 2,
        scratch_shapes=[
            pltpu.VMEM((ZS, 2, HIDDEN, PART), BF),
            pltpu.VMEM((RANK, ZS * BLOCK), F32),
            pltpu.VMEM((STEPS + 1, ZS, 2, 2, 2, RANK, TILE), BF),
            pltpu.VMEM((STEPS, 2, RANK, BOTH), F32),
            pltpu.VMEM((STEPS, 2, RANK, BOTH), F32),
            pltpu.VMEM((STEPS, 2, 2, RANK, BOTH), F32),
            pltpu.VMEM((STEPS, 2, 8, TILE), F32),
            pltpu.VMEM((STEPS, 8, TILE), F32),
            pltpu.VMEM((STEPS, ZS - 1, 8, TILE), F32),
            pltpu.VMEM((STEPS, ZS, 2, 2, RANK, TILE), F32),
            pltpu.VMEM((STEPS, ZS, 2, RANK, TILE), F32),
            pltpu.VMEM((STEPS, ZS, 2, 2, RANK, TILE), F32),
            pltpu.VMEM((STEPS, ZS, 2, 2, RANK, TILE), F32),
            pltpu.VMEM((STEPS, ZS, 2, RANK, TILE), F32),
            pltpu.VMEM((STEPS, ZS - 1, 2, RANK, TILE), F32),
            pltpu.VMEM((BOTH, TILE), F32),
            pltpu.SemaphoreType.REGULAR((4, 2)),
            dma((ZS,)), dma(()),
            dma((ZS,)), dma((ZS,)),
            dma((ZS // 2, 2)), dma((ZS // 2, 2)),
            dma((STEPS,)), dma((STEPS,)),
            dma((STEPS, 2, 2)), dma((STEPS, 2, 2)),
            dma((STEPS,)), dma((STEPS,)),
            dma((STEPS, ZS - 1)), dma((STEPS, ZS - 1)),
            dma((STEPS, ZS)), dma((STEPS, ZS)),
            dma((STEPS, ZS, 2, 2)), dma((STEPS, ZS, 2, 2)),
            dma((STEPS, ZS - 1)), dma((STEPS, ZS - 1)),
            dma((STEPS, ZS - 1)), dma((STEPS, ZS - 1)),
            dma((STEPS, ZS)), dma((STEPS, ZS)),
            dma((STEPS, ZS, 2, 2)), dma((STEPS, ZS, 2, 2)),
            dma((ZS,)), dma((ZS,)),
        ],
        compiler_params=pltpu.CompilerParams(
            collective_id=0, has_side_effects=True, vmem_limit_bytes=52 * 2**20
        ),
        cost_estimate=pl.CostEstimate(
            flops=10 * 32 * HIDDEN * 7168, bytes_accessed=HIDDEN * 7168 * 2, transcendentals=0
        ),
    )(*(pltpu.with_memory_space_constraint(x, pltpu.HBM) for x in (weights[0], factor_init[0])))
    new, nxt = pl.pallas_call(
        update_kernel,
        name="update",
        out_shape=(
            jax.ShapeDtypeStruct(weights.shape, BF),
            jax.ShapeDtypeStruct(factor_init.shape, F32),
        ),
        in_specs=[pl.BlockSpec(memory_space=pltpu.VMEM)] * 3,
        out_specs=[pl.BlockSpec(memory_space=pl.ANY)] * 2,
        scratch_shapes=[
            pltpu.VMEM((ZS, HIDDEN, BLOCK), BF),
            pltpu.VMEM((RANK, ZS * BLOCK), F32),
            pltpu.SemaphoreType.DMA((ZS,)),
            pltpu.SemaphoreType.DMA(()),
        ],
        compiler_params=pltpu.CompilerParams(vmem_limit_bytes=32 * 2**20),
        cost_estimate=pl.CostEstimate(
            flops=2 * 128 * HIDDEN * 7168, bytes_accessed=HIDDEN * 7168 * 4, transcendentals=0
        ),
    )(weights, lhs, fac)
    return new, nxt


def solution(mesh):
    in_specs = (P("group", "shard", None), P("group", None, None))
    out_specs = (P("group", "shard", None), P("group", None, None))
    return jax.shard_map(body, mesh=mesh, in_specs=in_specs, out_specs=out_specs, check_vma=False)
```

```python
import jax
import jax.numpy as jnp
from jax import lax
from jax.experimental import pallas as pl
from jax.experimental.pallas import tpu as pltpu
from jax.sharding import PartitionSpec as P

STEPS = 2
RANK = 16
gossip_rate = 0.5

BF = jnp.bfloat16
F32 = jnp.float32
MESH = pl.DeviceIdType.MESH

ZS = 8
BLOCK = 896
SKEW = 384
PART = 512
TILE = 128
HIDDEN = 320
BOTH = 640

ORDER = (4, 3, 5, 2, 6, 1, 7, 0)
NEAR = (0, 1, 7, 2, 6, 3, 5, 4)
GRAM_ON = 2
GRAM_AT = 4
ALL = tuple((d, e) for d in ORDER for e in (1, 0))
PEERS = tuple((d, e) for d in ORDER for e in (1, 0) if d or e)


def split3(x):
    hi = x.astype(BF)
    rest = x - hi.astype(F32)
    mid = rest.astype(BF)
    lo = (rest - mid.astype(F32)).astype(BF)
    return hi, mid, lo


def pack_gram(square):
    wide = jnp.concatenate([square, jnp.zeros((2 * RANK, TILE - 2 * RANK), F32)], axis=1)
    lane = lax.broadcasted_iota(jnp.int32, (8, TILE), 1)
    packed = jnp.where(lane < RANK, wide[:8], pltpu.roll(wide[8:16], RANK, axis=1))
    packed = jnp.where(lane < 2 * RANK, packed, pltpu.roll(wide[16:24], RANK, axis=1))
    return jnp.where(lane < 3 * RANK, packed, pltpu.roll(wide[24:], 2 * RANK, axis=1))


def inverse_factors(packed):
    rolled = [packed] + [pltpu.roll(packed, TILE - k * RANK, axis=1) for k in range(1, 4)]
    both = jnp.concatenate(rolled, axis=0).reshape(2, RANK, TILE)
    row = lax.broadcasted_iota(jnp.int32, (2, RANK, TILE), 1)
    lane = lax.broadcasted_iota(jnp.int32, (2, RANK, TILE), 2)
    eye = jnp.where(lane - RANK == row, 1.0, 0.0)
    a = jnp.where(lane < RANK, both, eye)
    for k in range(RANK - 1):
        pivot = a[:, k : k + 1, :]
        m = jnp.where(row[:, :, :1] > k, a[:, :, k : k + 1] / pivot[:, :, k : k + 1], 0.0)
        a = a - m * pivot
    diagonal = jnp.sum(jnp.where(lane == row, a, 0.0), axis=2, keepdims=True)
    return a / jnp.sqrt(diagonal)


def apply_lower(inverse, x):
    total = inverse[:, RANK : RANK + 1] * x[0:1, :]
    for k in range(1, RANK):
        total = total + inverse[:, RANK + k : RANK + k + 1] * x[k : k + 1, :]
    return total


def main_kernel(
    w_hbm, f0_hbm, lhs_ref, fac_ref,
    w, f0, f, xs, xc, xr, gs, gx, gz, ko, kx, sn, rn, dd, r, bt,
    hop, w_sem, f0_sem, wx_s, wx_r, init_s, init_r, c_s, c_r, x_s, x_r, gx_s, gx_r, gz_s, gz_r,
    k_s, k_r, p_s, p_r, r_s, r_r, az_s, az_r, ax_s, ax_r, ag_s, ag_r, ac_s, ac_r,
):
    g = lax.axis_index("group")
    s = lax.axis_index("shard")
    z, xh, c = s // 4, (s // 2) % 2, s % 2
    other = (g, s + 1 - 2 * c)
    left, right = ((g + 7) % 8, s), ((g + 1) % 8, s)

    def peer(d, e):
        return (g, ((z + d) % ZS) * 4 + ((xh + e) % 2) * 2 + c)

    started = []

    def send(src, dst, ss, rs, to):
        copy = pltpu.make_async_remote_copy(
            src_ref=src, dst_ref=dst, send_sem=ss, recv_sem=rs, device_id=to, device_id_type=MESH
        )
        copy.start()
        started.append(copy)
        return copy

    def settle():
        while started:
            started.pop(0).wait_send()

    def columns(b, core):
        return pl.ds(pl.multiple_of(b * BLOCK + core * SKEW, TILE), PART)

    beyond = [((g + k) % 8, s + 1 - 2 * c) for k in (7, 1)]
    f0_load = pltpu.make_async_copy(f0_hbm, f0, f0_sem)
    f0_load.start()
    barrier = pltpu.get_barrier_semaphore()
    above, below = peer(1, 0), peer(7, 0)
    aside = [((g + k) % 8, peer(0, 1)[1]) for k in (7, 1)]
    greeted = [other, left, right, above, below, peer(0, 1)] + beyond + aside
    for device in greeted:
        pl.semaphore_signal(barrier, inc=1, device_id=device, device_id_type=MESH)

    loads = []
    for b in range(ZS):
        load = pltpu.make_async_copy(w_hbm.at[:, columns(b, c)], w.at[b, c], w_sem.at[b])
        load.start()
        loads.append(load)

    def tell(k):
        for way, device in enumerate((above, below)):
            pl.semaphore_signal(hop.at[k, way], inc=1, device_id=device, device_id_type=MESH)

    def hear(k):
        for way in range(2):
            pl.semaphore_wait(hop.at[k, way], 1)

    pl.semaphore_wait(barrier, len(greeted))
    tell(0)

    swaps = [
        send(w_hbm.at[:, columns(b, 1 - c)], w.at[b, c], wx_s.at[b], wx_r.at[b], other)
        for b in range(ZS)
    ]

    f0_load.wait()
    first = []
    for b in range(ZS):
        for t in range(4):
            tile = pl.ds(pl.multiple_of(b * BLOCK + c * SKEW + t * TILE, TILE), TILE)
            f[0, b, t // 2, t % 2, 1] = f0[:, tile].astype(BF)
        if b % 2:
            two = pl.ds(b - 1, 2)
            first.append([
                send(
                    f.at[0, two, k, :, 1], f.at[0, two, 1 - k, :, 0],
                    init_s.at[b // 2, k], init_r.at[b // 2, 1 - k], right,
                )
                for k in range(2)
            ])

    for k in range(2):
        hear(k)
        tell(k + 1)
    gathers = {}
    for step in range(STEPS):
        part = jnp.zeros((2 * RANK, BOTH), F32)
        for i, d in enumerate(NEAR):
            if step == 0:
                b = i
                if i == 4:
                    hear(2)
                    tell(3)
                loads[b].wait()
                swaps[b].wait_recv()
                if b % 2 == 0:
                    for copy in first[b // 2]:
                        copy.wait_recv()
            else:
                b = (z + ZS - d) % ZS
                for copy in gathers[d]:
                    copy.wait_recv()
            tiles = []
            for t in range(4):
                k = t // 2
                tile = jnp.concatenate([f[step, b, 1 - k, t % 2, 0], f[step, b, k, t % 2, 1]], axis=0)
                if t == 0:
                    tile = jnp.where(c == 1, jnp.zeros_like(tile), tile)
                tiles.append(tile)
            part = part + lax.dot_general(
                jnp.concatenate(tiles, axis=1), w[b].reshape(BOTH, PART),
                (((1,), (1,)), ((), ())), preferred_element_type=F32,
            )
        xs[step, 0] = part[:RANK]
        xs[step, 1] = part[RANK:]
        swapped = [
            send(xs.at[step, side], xr.at[step, far, 1 - side], x_s.at[step, far, side], x_r.at[step, far, 1 - side], to)
            for side, same in ((1, right), (0, left))
            for far, to in ((0, same), (1, beyond[side]))
        ]
        swapped.append(send(xs.at[step], xc.at[step], c_s.at[step], c_r.at[step], other))
        for copy in swapped:
            copy.wait_recv()
        raw = jnp.concatenate([
            (xr[step, 0, 0] + xr[step, 1, 0]) - (part[:RANK] + xc[step, 0]),
            (part[RANK:] + xc[step, 1]) - (xr[step, 0, 1] + xr[step, 1, 1]),
        ], axis=0)

        stacked = jnp.concatenate(split3(raw), axis=0)
        cross_copies = []
        for i, d in enumerate(ORDER):
            b = (z + d) % ZS
            prod = jnp.dot(stacked, w[b].reshape(BOTH, PART), preferred_element_type=F32)
            prod = prod[: 2 * RANK] + (prod[2 * RANK : 4 * RANK] + prod[4 * RANK :])
            for t in range(2):
                own, over = slice(t * TILE, (t + 1) * TILE), slice((2 + t) * TILE, (3 + t) * TILE)
                ko[step, i, t, 0] = -prod[:RANK, over]
                ko[step, i, t, 1] = prod[RANK:, own]
                sn[step, i, 0, t] = -prod[:RANK, own]
                sn[step, i, 1, t] = prod[RANK:, over]
            cross_copies.append([
                send(ko.at[step, i, 1 - xh], kx.at[step, i], k_s.at[step, i], k_r.at[step, i], peer(0, 1))
            ] + [
                send(
                    sn.at[step, i, side, (xh + far) % 2], rn.at[step, i, far, 1 - side],
                    p_s.at[step, i, far, side], p_r.at[step, i, far, 1 - side], to,
                )
                for far, pair in ((0, (left, right)), (1, aside))
                for side, to in enumerate(pair)
            ])
            if i == GRAM_AT:
                if step == 0:
                    hear(3)
                square = lax.dot_general(
                    raw, raw, (((1,), (1,)), ((), ())),
                    precision=lax.Precision.HIGHEST, preferred_element_type=F32,
                )
                gram = pack_gram(square)
                gs[step, 0] = gram
                gram_x = send(gs.at[step, 0], gx.at[step], gx_s.at[step], gx_r.at[step], peer(0, 1))

        reduce_copies = []
        for i, d in enumerate(ORDER):
            if i == GRAM_ON:
                gram_x.wait_recv()
                gram = gram + gx[step]
                gs[step, 1] = gram
                gram_copies = [
                    send(gs.at[step, 1], gz.at[step, j], gz_s.at[step, j], gz_r.at[step, j], peer(d2, 0))
                    for j, d2 in enumerate(ORDER[:-1])
                ]
            for copy in cross_copies[i]:
                copy.wait_recv()
            dd[step, i] = ko[step, i, xh] + kx[step, i] + (rn[step, i, 0] + rn[step, i, 1])
            if d:
                reduce_copies.append(send(
                    dd.at[step, i], r.at[step, i], r_s.at[step, i], r_r.at[step, i], peer(d, 0)
                ))

        for j, copy in enumerate(gram_copies):
            copy.wait_recv()
            gram = gram + gz[step, j]
        inverses = inverse_factors(gram)

        total = dd[step, ZS - 1]
        for j, copy in enumerate(reduce_copies):
            copy.wait_recv()
            total = total + r[step, j]

        f[step + 1, z, 0, xh, 0] = apply_lower(inverses[0], total[0]).astype(BF)
        f[step + 1, z, 0, xh, 1] = apply_lower(inverses[1], total[1]).astype(BF)
        piece = f.at[step + 1, z, 0, xh]
        early = len(started)
        along = {
            d: send(piece, piece, az_s.at[step, j], az_r.at[step, j], peer(d, 0))
            for j, d in enumerate(ORDER[:-1])
        }
        for copy in started[:early]:
            copy.wait_send()
        del started[:early]
        if step == STEPS - 1:
            basis = gossip_rate * jnp.concatenate(
                [-apply_lower(inverses[0], raw[:RANK]), apply_lower(inverses[1], raw[RANK:])], axis=0
            )
            terms = [term.astype(F32) for term in split3(basis)]
            bt[...] = jnp.concatenate(terms + [jnp.zeros((2 * RANK, BOTH), F32)], axis=0).T
            lhs_ref[...] = bt[pl.ds(pl.multiple_of(c * HIDDEN, 16), HIDDEN), :].astype(BF)
        gathers = {}
        for i, d in enumerate(NEAR):
            if d:
                along[d].wait_recv()
            b = (z + ZS - d) % ZS
            here = f.at[step + 1, b, 0, xh]
            gathers[d] = [
                send(
                    here.at[side], f.at[step + 1, b, 1, xh, 1 - side],
                    ag_s.at[step, i, far, side], ag_r.at[step, i, far, 1 - side], to,
                )
                for far, pair in ((0, (left, right)), (1, aside))
                for side, to in enumerate(pair)
            ] + [send(here, here, ax_s.at[step, i], ax_r.at[step, i], peer(0, 1))]

    lasts = []
    for i, d in enumerate(NEAR):
        b = (z + ZS - d) % ZS
        for copy in gathers[d]:
            copy.wait_recv()
        lasts.append(send(f.at[STEPS, b], fac_ref.at[c, b], ac_s.at[i], ac_r.at[i], other))
        fac_ref[c, b] = f[STEPS, b]
    settle()
    for copy in lasts:
        copy.wait_recv()


def update_kernel(w_ref, lhs_ref, fac_ref, new_hbm, next_hbm, new, nxt, new_sem, next_sem):
    stores = []
    for b in range(ZS):
        tiles = []
        for core in range(2):
            for t in range(core, 4):
                k = t // 2
                tiles.append(jnp.concatenate(
                    [fac_ref[core, b, 1 - k, t % 2, 0], fac_ref[core, b, k, t % 2, 1]], axis=0
                ))
        fac = jnp.concatenate(tiles, axis=1)
        rhs = jnp.concatenate([fac, fac, fac, jnp.zeros_like(fac)], axis=0)
        delta = jnp.dot(lhs_ref[...], rhs, preferred_element_type=F32)
        columns = slice(b * BLOCK, (b + 1) * BLOCK)
        new[b] = (w_ref[0, :, columns].astype(F32) - delta).astype(BF)
        store = pltpu.make_async_copy(new.at[b], new_hbm.at[0, :, columns], new_sem.at[b])
        store.start()
        stores.append(store)
        nxt[:, columns] = fac[RANK:].astype(F32)
    store = pltpu.make_async_copy(nxt, next_hbm.at[0], next_sem)
    store.start()
    for copy in [*stores, store]:
        copy.wait()


def body(weights, factor_init):
    dma = pltpu.SemaphoreType.DMA
    n = len(PEERS)
    lhs, fac = pl.pallas_call(
        main_kernel,
        name="rounds",
        out_shape=(
            jax.ShapeDtypeStruct((HIDDEN, TILE), BF),
            jax.ShapeDtypeStruct((2, ZS, 2, 2, 2, RANK, TILE), BF),
        ),
        in_specs=[pl.BlockSpec(memory_space=pltpu.HBM)] * 2,
        out_specs=[pl.BlockSpec(memory_space=pltpu.VMEM)] * 2,
        scratch_shapes=[
            pltpu.VMEM((ZS, 2, HIDDEN, PART), BF),
            pltpu.VMEM((RANK, ZS * BLOCK), F32),
            pltpu.VMEM((STEPS + 1, ZS, 2, 2, 2, RANK, TILE), BF),
            pltpu.VMEM((STEPS, 2, RANK, BOTH), F32),
            pltpu.VMEM((STEPS, 2, RANK, BOTH), F32),
            pltpu.VMEM((STEPS, 2, 2, RANK, BOTH), F32),
            pltpu.VMEM((STEPS, 2, 8, TILE), F32),
            pltpu.VMEM((STEPS, 8, TILE), F32),
            pltpu.VMEM((STEPS, ZS - 1, 8, TILE), F32),
            pltpu.VMEM((STEPS, ZS, 2, 2, RANK, TILE), F32),
            pltpu.VMEM((STEPS, ZS, 2, RANK, TILE), F32),
            pltpu.VMEM((STEPS, ZS, 2, 2, RANK, TILE), F32),
            pltpu.VMEM((STEPS, ZS, 2, 2, RANK, TILE), F32),
            pltpu.VMEM((STEPS, ZS, 2, RANK, TILE), F32),
            pltpu.VMEM((STEPS, ZS - 1, 2, RANK, TILE), F32),
            pltpu.VMEM((BOTH, TILE), F32),
            pltpu.SemaphoreType.REGULAR((4, 2)),
            dma((ZS,)), dma(()),
            dma((ZS,)), dma((ZS,)),
            dma((ZS // 2, 2)), dma((ZS // 2, 2)),
            dma((STEPS,)), dma((STEPS,)),
            dma((STEPS, 2, 2)), dma((STEPS, 2, 2)),
            dma((STEPS,)), dma((STEPS,)),
            dma((STEPS, ZS - 1)), dma((STEPS, ZS - 1)),
            dma((STEPS, ZS)), dma((STEPS, ZS)),
            dma((STEPS, ZS, 2, 2)), dma((STEPS, ZS, 2, 2)),
            dma((STEPS, ZS - 1)), dma((STEPS, ZS - 1)),
            dma((STEPS, ZS - 1)), dma((STEPS, ZS - 1)),
            dma((STEPS, ZS)), dma((STEPS, ZS)),
            dma((STEPS, ZS, 2, 2)), dma((STEPS, ZS, 2, 2)),
            dma((ZS,)), dma((ZS,)),
        ],
        compiler_params=pltpu.CompilerParams(
            collective_id=0, has_side_effects=True, vmem_limit_bytes=52 * 2**20
        ),
        cost_estimate=pl.CostEstimate(
            flops=10 * 32 * HIDDEN * 7168, bytes_accessed=HIDDEN * 7168 * 2, transcendentals=0
        ),
    )(*(pltpu.with_memory_space_constraint(x, pltpu.HBM) for x in (weights[0], factor_init[0])))
    new, nxt = pl.pallas_call(
        update_kernel,
        name="update",
        out_shape=(
            jax.ShapeDtypeStruct(weights.shape, BF),
            jax.ShapeDtypeStruct(factor_init.shape, F32),
        ),
        in_specs=[pl.BlockSpec(memory_space=pltpu.VMEM)] * 3,
        out_specs=[pl.BlockSpec(memory_space=pl.ANY)] * 2,
        scratch_shapes=[
            pltpu.VMEM((ZS, HIDDEN, BLOCK), BF),
            pltpu.VMEM((RANK, ZS * BLOCK), F32),
            pltpu.SemaphoreType.DMA((ZS,)),
            pltpu.SemaphoreType.DMA(()),
        ],
        compiler_params=pltpu.CompilerParams(vmem_limit_bytes=32 * 2**20),
        cost_estimate=pl.CostEstimate(
            flops=2 * 128 * HIDDEN * 7168, bytes_accessed=HIDDEN * 7168 * 4, transcendentals=0
        ),
    )(weights, lhs, fac)
    return new, nxt


def solution(mesh):
    in_specs = (P("group", "shard", None), P("group", None, None))
    out_specs = (P("group", "shard", None), P("group", None, None))
    return jax.shard_map(body, mesh=mesh, in_specs=in_specs, out_specs=out_specs, check_vma=False)
```
